256 devices in a mesh: dom: 32 (over x, y, z_hi), edge: 8 (over z_lo, core).
Axes of the slice: x: 4, y: 4, z: 8 (z_hi: 2, z_lo: 4; z = z_hi * 4 + z_lo), core: 2. Of those that a mesh axis runs over, the one named last changes fastest.
Arguments:
- node_lat: bfloat16 [65536, 256], P(('dom', 'edge')), may hold values from -6 to 6
- edge_lat: bfloat16 [786432, 256], P(('dom', 'edge')), may hold values from -6 to 6
- senders: int32 [786432], P(('dom', 'edge')), may hold values from 0 to 6143
- receivers: int32 [786432], P(('dom', 'edge')), may hold values from 0 to 2047
- live_edges: int32 [32, 8], P('dom', 'edge'), may hold values from 768 to 3072, as said below
- send_rows: int32 [256, 4, 128], P(('dom', 'edge')), may hold values from 0 to 255, as said below
- edge_w1: bfloat16 [2, 768, 256], replicated, may hold values from -0.21875 to 0.21875
- edge_b1: float32 [2, 256], replicated, may hold values from -3 to 3
- edge_w2: bfloat16 [2, 256, 256], replicated, may hold values from -0.375 to 0.375
- edge_gain: float32 [2, 256], replicated, may hold values from 0.1 to 1.9
- node_w1: bfloat16 [2, 512, 256], replicated, may hold values from -0.25 to 0.25
- node_b1: float32 [2, 256], replicated, may hold values from -3 to 3
- node_w2: bfloat16 [2, 256, 256], replicated, may hold values from -0.375 to 0.375
- node_gain: float32 [2, 256], replicated, may hold values from 0.1 to 1.9
Outputs:
- node_out: bfloat16 [65536, 256], P(('dom', 'edge'))
- edge_out: bfloat16 [786432, 256], P(('dom', 'edge'))
The draws below stay inside these ranges and needn't reach their ends.
Inputs may be any that keep to these rules, and one draw needn't show every extreme that they name: `send_rows`: for each device and face, 128 distinct rows of the device's own 256 nodes. `live_edges`: a multiple of 128 for every device; some device is full in every draw. `senders`: rows of the domain's node table. `receivers`: nodes of the edge's own domain.
All inputs are finite; a program needn't handle non-finite values.
Results may differ from the reference program's by a relative error of at most 0.014.
Values may be sent and summed in bfloat16 or wider, within the bound.
A program may use at most 64 MiB of HBM per device.

```python
import jax
import jax.numpy as jnp
from jax import lax

LATENT = 256
HIDDEN_SIZE = 256
NODE_DEV = 256
EDGE_DEV = 3072
HALO_DEV = 128
BLOCK = 128
LAYERS = 2
FACES = 4
NODE_DOM = 2048
TABLE_ROWS = 6144
NODES = 65536
EDGES = 786432
N_DOM = 32
N_EDGE = 8


def draw_live_edges(key, part):
    block_total = EDGE_DEV // BLOCK
    lowest = max(1, block_total // 4)
    first_key, second_key = jax.random.split(key)
    block_counts = jax.random.randint(first_key, (N_DOM * N_EDGE,), lowest, block_total + 1)
    full_device = jax.random.randint(second_key, (), 0, N_DOM * N_EDGE)
    block_counts = jnp.where(jnp.arange(N_DOM * N_EDGE) == full_device, block_total, block_counts)
    return (block_counts * BLOCK).reshape(N_DOM, N_EDGE).astype(jnp.int32)


def draw_send_rows(key, part):
    list_total = N_DOM * N_EDGE * FACES
    key_list = jax.random.split(key, list_total)

    def pick_rows(one_key):
        return jax.random.permutation(one_key, NODE_DEV)[:HALO_DEV]
    picked = jax.vmap(pick_rows)(key_list)
    return picked.reshape(N_DOM * N_EDGE, FACES, HALO_DEV).astype(jnp.int32)


def touch_ends(entries, rng, least, top_value):
    extent = entries.shape
    spot = [jax.random.randint(jax.random.fold_in(rng, axis), (), 0, extent[axis]) for axis in range(len(extent))]
    entries = entries.at[tuple(spot)].set(least)
    longest = extent.index(max(extent))
    spot[longest] = (spot[longest] + 1) % extent[longest]
    return entries.at[tuple(spot)].set(top_value)


def block_levels(rng, shape, pieces, least, high):
    gain, own = 1.0, jax.random.fold_in(rng, 6)
    for dim, blocks in pieces:
        draws = jnp.exp(jax.random.uniform(jax.random.fold_in(own, dim), (blocks,), jnp.float32, least / len(pieces), high / len(pieces)))
        gain = gain * jnp.repeat(draws, shape[dim] // blocks).reshape([-1 if axis == dim else 1 for axis in range(len(shape))])
    return gain


def gaussian(key, extent, scale, most, shards=(), held_as=jnp.bfloat16):
    entries = jax.random.normal(key, extent, jnp.float32) * scale
    if len(shards) > 0:
        entries = block_levels(key, extent, shards, -0.22, 0.18) * entries
    return jnp.clip(entries, min=-most, max=most).astype(held_as)


def setup_inputs(seed: int = 0) -> dict:
    key_of = jax.random.split(jax.random.key(seed), 15)
    return {
        "node_lat": gaussian(key_of[0], (NODES, LATENT), 1.0, 6.0, ((0, 256),)),
        "edge_lat": gaussian(key_of[1], (EDGES, LATENT), 1.0, 6.0, ((0, 256),)),
        "senders": touch_ends(jax.random.randint(key_of[2], (EDGES,), 0, TABLE_ROWS), jax.random.fold_in(key_of[2], 1), 0, TABLE_ROWS - 1).astype(jnp.int32),
        "receivers": touch_ends(jax.random.randint(key_of[3], (EDGES,), 0, NODE_DOM), jax.random.fold_in(key_of[3], 1), 0, NODE_DOM - 1).astype(jnp.int32),
        "live_edges": draw_live_edges(jax.random.fold_in(key_of[14], 71), 0),
        "send_rows": draw_send_rows(jax.random.fold_in(key_of[14], 71), 0),
        "edge_w1": gaussian(key_of[6], (LAYERS, 3 * LATENT, HIDDEN_SIZE), (3 * LATENT) ** -0.5, 0.21875),
        "edge_b1": gaussian(key_of[7], (LAYERS, HIDDEN_SIZE), 0.5, 3.0, (), jnp.float32),
        "edge_w2": gaussian(key_of[8], (LAYERS, HIDDEN_SIZE, LATENT), HIDDEN_SIZE ** -0.5, 0.375),
        "edge_gain": jnp.clip(1.0 + 0.18 * jax.random.normal(key_of[9], (LAYERS, LATENT), jnp.float32), 0.1, 1.9),
        "node_w1": gaussian(key_of[10], (LAYERS, 2 * LATENT, HIDDEN_SIZE), (2 * LATENT) ** -0.5, 0.25),
        "node_b1": gaussian(key_of[11], (LAYERS, HIDDEN_SIZE), 0.5, 3.0, (), jnp.float32),
        "node_w2": gaussian(key_of[12], (LAYERS, HIDDEN_SIZE, LATENT), HIDDEN_SIZE ** -0.5, 0.375),
        "node_gain": jnp.clip(1.0 + 0.18 * jax.random.normal(key_of[13], (LAYERS, LATENT), jnp.float32), 0.1, 1.9),
    }


eps_norm = 1e-05

def layer_norm(values, norm_gain):
    center = values - lax.optimization_barrier(jnp.mean(values, axis=-1, keepdims=True))
    spread = lax.optimization_barrier(jnp.mean(center * center, axis=-1, keepdims=True))
    return center * lax.rsqrt(spread + eps_norm) * norm_gain.astype(jnp.float32)

def edge_update(edge_rows, sender_rows, receiver_rows, weight_in, bias_in, weight_out, norm_gain, live_rows):
    feature_width = edge_rows.shape[1]
    pre_act = jnp.dot(edge_rows, weight_in[:feature_width], preferred_element_type=jnp.float32)
    pre_act = pre_act + jnp.dot(sender_rows, weight_in[feature_width:2 * feature_width], preferred_element_type=jnp.float32)
    pre_act = pre_act + jnp.dot(receiver_rows, weight_in[2 * feature_width:], preferred_element_type=jnp.float32)
    hidden_rows = jax.nn.relu(pre_act + bias_in.astype(jnp.float32)).astype(jnp.bfloat16)
    messages = layer_norm(jnp.dot(hidden_rows, weight_out, preferred_element_type=jnp.float32), norm_gain)
    messages = jnp.where(live_rows[:, None], messages, jnp.float32(0.0))
    return ((edge_rows.astype(jnp.float32) + messages).astype(jnp.bfloat16), messages)

def node_update(node_rows, aggregate, weight_in, bias_in, weight_out, norm_gain):
    feature_width = node_rows.shape[1]
    pre_act = jnp.dot(node_rows, weight_in[:feature_width], preferred_element_type=jnp.float32)
    pre_act = pre_act + jnp.dot(aggregate, weight_in[feature_width:], preferred_element_type=jnp.float32)
    hidden_rows = jax.nn.relu(pre_act + bias_in.astype(jnp.float32)).astype(jnp.bfloat16)
    update = layer_norm(jnp.dot(hidden_rows, weight_out, preferred_element_type=jnp.float32), norm_gain)
    return (node_rows.astype(jnp.float32) + update).astype(jnp.bfloat16)

def reference(node_lat, edge_lat, senders, receivers, live_edges, send_rows, edge_w1, edge_b1, edge_w2, edge_gain, node_w1, node_b1, node_w2, node_gain):
    stride = N_DOM // 4
    offsets = (1, -1, stride, -stride)
    node_dom = N_EDGE * NODE_DEV
    rank_base = (jnp.arange(N_DOM * N_EDGE, dtype=jnp.int32) * NODE_DEV)[:, None, None]
    picks = (send_rows + rank_base).astype(jnp.int32).reshape(N_DOM, N_EDGE, FACES, HALO_DEV)
    live_all = jnp.arange(EDGE_DEV, dtype=jnp.int32)[None, None, :] < live_edges[:, :, None]
    live_all = live_all.reshape(N_DOM, N_EDGE * EDGE_DEV)
    sender_dom = senders.reshape(N_DOM, N_EDGE * EDGE_DEV)
    receiver_dom = receivers.reshape(N_DOM, N_EDGE * EDGE_DEV)
    owned_rows = node_lat
    edge_rows = edge_lat
    for layer_index in range(LAYERS):
        sent = jnp.take(owned_rows, picks, axis=0)
        received = jnp.stack([jnp.roll(sent[:, :, face_index], offsets[face_index], axis=0) for face_index in range(FACES)], axis=2)
        halo_all = received.reshape(N_DOM, N_EDGE * FACES * HALO_DEV, LATENT)
        domain_rows = owned_rows.reshape(N_DOM, node_dom, LATENT)
        node_table = jnp.concatenate([domain_rows, halo_all], axis=1)
        edge_dom = edge_rows.reshape(N_DOM, N_EDGE * EDGE_DEV, LATENT)

        def one_domain(items):
            table_one, domain_one, edges_one, send_one, recv_one, live_one = items
            new_edges, messages = edge_update(edges_one, jnp.take(table_one, send_one, axis=0), jnp.take(domain_one, recv_one, axis=0), edge_w1[layer_index], edge_b1[layer_index], edge_w2[layer_index], edge_gain[layer_index], live_one)
            message_parts = messages.reshape(N_EDGE, EDGE_DEV, LATENT)
            recv_parts = recv_one.reshape(N_EDGE, EDGE_DEV)
            summed = jnp.zeros((node_dom, LATENT), jnp.float32)
            for rank_index in range(N_EDGE):
                partial_sum = jax.ops.segment_sum(message_parts[rank_index], recv_parts[rank_index], num_segments=node_dom)
                rounded = lax.optimization_barrier(partial_sum.astype(jnp.bfloat16))
                summed = summed + rounded.astype(jnp.float32)
            return (new_edges, summed.astype(jnp.bfloat16))
        new_edges, aggregate = lax.map(one_domain, (node_table, domain_rows, edge_dom, sender_dom, receiver_dom, live_all))
        edge_rows = new_edges.reshape(-1, LATENT)
        owned_rows = node_update(owned_rows, aggregate.reshape(-1, LATENT), node_w1[layer_index], node_b1[layer_index], node_w2[layer_index], node_gain[layer_index])
    return (owned_rows, edge_rows)
```

```python
import functools

import jax
import jax.numpy as jnp
from jax import lax
from jax.experimental import pallas as pl
from jax.experimental.pallas import tpu as pltpu
from jax.sharding import PartitionSpec as P

LAYERS = 2
EPS = 1e-05
FACES = 4
HALO = 128
GROUP = 32
MESH = pl.DeviceIdType.MESH
BF16 = jnp.bfloat16
F32 = jnp.float32


def dot(a, b):
    return jnp.dot(a, b, preferred_element_type=F32)


def layer_norm(values, gain):
    center = values - jnp.mean(values, axis=-1, keepdims=True)
    spread = jnp.mean(center * center, axis=-1, keepdims=True)
    return center * lax.rsqrt(spread + EPS) * gain


def edge_kernel(
    live_ref,
    send_ref,
    recv_ref,
    recv_row_ref,
    table_ref,
    edge_ref,
    w1_ref,
    b1_ref,
    w2_ref,
    gain_ref,
    edge_out_ref,
    part_ref,
    s_ref,
    r_ref,
    pre_ref,
    msg_ref,
):
    nodes = part_ref.shape[0]
    rows = table_ref.shape[0]
    edges, width = edge_ref.shape
    half = width // 2
    step = 512
    chunk = 256

    @pl.loop(0, rows // step)
    def _(i):
        base = pl.multiple_of(i * step, step)
        val = dot(table_ref[pl.ds(base, step), :], w1_ref[width : 2 * width, :])
        s_ref[pl.ds(2 * base, step, stride=2), :] = val[:, :half]
        s_ref[pl.ds(2 * base + 1, step, stride=2), :] = val[:, half:]

    @pl.loop(0, nodes // step)
    def _(i):
        base = pl.multiple_of(i * step, step)
        val = dot(table_ref[pl.ds(base, step), :], w1_ref[2 * width :, :]) + b1_ref[...]
        r_ref[pl.ds(2 * base, step, stride=2), :] = val[:, :half]
        r_ref[pl.ds(2 * base + 1, step, stride=2), :] = val[:, half:]

    live = live_ref[0, 0]

    @pl.loop(0, edges // chunk)
    def _(i):
        base = pl.multiple_of(i * chunk, chunk)

        @pl.loop(0, chunk // GROUP)
        def _(g):
            for u in range(GROUP):
                k = base + g * GROUP + u
                a = send_ref[k]
                b = recv_ref[k]
                at = pl.multiple_of(g * (2 * GROUP), 2 * GROUP) + 2 * u
                pre_ref[pl.ds(at, 2), :] = (
                    s_ref[pl.ds(pl.multiple_of(2 * a, 2), 2), :]
                    + r_ref[pl.ds(pl.multiple_of(2 * b, 2), 2), :]
                )

        old = edge_ref[pl.ds(base, chunk), :]
        pre = dot(old, w1_ref[:width, :])
        low = pre[:, :half] + pre_ref[pl.ds(0, chunk, stride=2), :]
        high = pre[:, half:] + pre_ref[pl.ds(1, chunk, stride=2), :]
        hidden = jnp.maximum(jnp.concatenate([low, high], axis=1), 0.0).astype(BF16)
        message = layer_norm(dot(hidden, w2_ref[...]), gain_ref[...])
        slot = lax.broadcasted_iota(jnp.int32, (chunk, 1), 0) + base
        message = jnp.where(slot < live, message, 0.0)
        edge_out_ref[pl.ds(base, chunk), :] = (old.astype(F32) + message).astype(BF16)
        msg_ref[pl.ds(base, chunk), :] = message.astype(BF16)

    nb = 256
    kb = 512

    @pl.loop(0, nodes // nb)
    def _(i):
        base = pl.multiple_of(i * nb, nb)
        ids = lax.broadcasted_iota(jnp.int32, (nb, kb), 0) + base
        acc = jnp.zeros((nb, width), F32)
        for j in range(edges // kb):
            hit = ids == recv_row_ref[:, j * kb : (j + 1) * kb]
            acc = acc + dot(
                jnp.where(hit, 1.0, 0.0).astype(BF16), msg_ref[j * kb : (j + 1) * kb, :]
            )
        part_ref[pl.ds(base, nb), :] = acc.astype(BF16)


def edge_step(table, edges, senders, receivers, live, w1, b1, w2, gain, nodes):
    vmem = pl.BlockSpec(memory_space=pltpu.VMEM)
    smem = pl.BlockSpec(memory_space=pltpu.SMEM)
    rows, width = table.shape
    count = edges.shape[0]
    return pl.pallas_call(
        edge_kernel,
        out_shape=(
            jax.ShapeDtypeStruct(edges.shape, BF16),
            jax.ShapeDtypeStruct((nodes, width), BF16),
        ),
        in_specs=[smem, smem, smem] + [vmem] * 7,
        out_specs=(vmem, vmem),
        scratch_shapes=[
            pltpu.VMEM((2 * rows, width // 2), F32),
            pltpu.VMEM((2 * nodes, width // 2), F32),
            pltpu.VMEM((2 * 256, width // 2), F32),
            pltpu.VMEM((count, width), BF16),
        ],
        compiler_params=pltpu.CompilerParams(vmem_limit_bytes=48 * 2**20),
        cost_estimate=pl.CostEstimate(
            flops=12 * 10**9, bytes_accessed=9 * 2**20, transcendentals=0
        ),
        name="edge_step",
    )(live, senders, receivers, receivers.reshape(1, -1), table, edges, w1, b1, w2, gain)


def node_kernel(reduce, spread, *refs):
    refs = list(refs)
    own_ref = refs.pop(0)
    if reduce:
        part_ref, w1_ref, b1_ref, w2_ref, gain_ref = (refs.pop(0) for _ in range(5))
    if spread:
        list_ref = refs.pop(0)
    if reduce:
        node_out_ref = refs.pop(0)
    if spread:
        table_ref = refs.pop(0)
    if reduce:
        pair_ref, sums_ref, got_ref = (refs.pop(0) for _ in range(3))
        pair_sem, sum_sem = (refs.pop(0) for _ in range(2))
    if spread:
        lists_ref, zface_ref, xface_ref = (refs.pop(0) for _ in range(3))
        list_sem, node_sem, zf_sem, xf_sem, fn_sem, fz_sem, fx_sem = (
            refs.pop(0) for _ in range(7)
        )

    d = lax.axis_index("dom")
    e = lax.axis_index("edge")
    doms = lax.axis_size("dom")
    count = lax.axis_size("edge")
    chips = count // 2
    stride = doms // 4
    size, width = own_ref.shape
    q = e // 2
    c = e % 2
    sib = 2 * q + 1 - c

    def peer(t):
        return 2 * ((q + t) % chips) + c

    def source(t):
        return 2 * ((q - t + chips) % chips) + c

    offsets = (1, doms - 1, stride, doms - stride)
    there = [(d + s) % doms for s in offsets]

    barrier = pltpu.get_barrier_semaphore()
    greet = [(d, sib)] + [(d, peer(t)) for t in range(1, chips)]
    if spread:
        greet += [(there[f], peer(t)) for f in range(2) for t in range(chips)]
        greet += [(there[f], e) for f in range(2, 4)]
    for who in greet:
        pl.semaphore_signal(barrier, inc=1, device_id=who, device_id_type=MESH)
    pl.semaphore_wait(barrier, len(greet))

    def send(src, dst, sems, index, who):
        copy = pltpu.make_async_remote_copy(
            src_ref=src,
            dst_ref=dst,
            send_sem=sems.at[(0,) + index],
            recv_sem=sems.at[(1,) + index],
            device_id=who,
            device_id_type=MESH,
        )
        copy.start()
        return copy

    sent = []
    own = own_ref[...]

    if spread:
        lists_ref[0] = list_ref[...]
        got_lists = [None]
        for t in range(1, chips):
            copy = send(list_ref, lists_ref.at[t], list_sem, (t,), (d, peer(t)))
            got_lists.append(copy)

    if reduce:
        pairs = []
        for t in range(chips - 1, -1, -1):
            block = 2 * ((q + t) % chips) + 1 - c
            copy = send(
                part_ref.at[pl.ds(pl.multiple_of(block * size, size), size), :],
                pair_ref.at[t],
                pair_sem,
                (t,),
                (d, sib),
            )
            pairs.append((t, copy))
        moved = []
        mine = None
        for t, copy in pairs:
            copy.wait_recv()
            at = pl.multiple_of(peer(t) * size, size)
            total = part_ref[pl.ds(at, size), :].astype(F32) + pair_ref[t].astype(F32)
            if t:
                sums_ref[t] = total.astype(BF16)
                moved.append(send(sums_ref.at[t], got_ref.at[t], sum_sem, (t,), (d, peer(t))))
            else:
                mine = total
            sent.append(copy)
        pre = dot(own, w1_ref[:width, :]) + b1_ref[...]
        for t, copy in zip(range(chips - 1, 0, -1), moved):
            copy.wait_recv()
            mine = mine + got_ref[t].astype(F32)
            sent.append(copy)
        pre = pre + dot(mine.astype(BF16), w1_ref[width:, :])
        hidden = jnp.maximum(pre, 0.0).astype(BF16)
        update = layer_norm(dot(hidden, w2_ref[...]), gain_ref[...])
        own = (own.astype(F32) + update).astype(BF16)
        node_out_ref[...] = own

    if spread:
        nodes = count * size

        def node_at(owner):
            return table_ref.at[pl.ds(pl.multiple_of(owner * size, size), size), :]

        def halo_at(owner, f):
            at = nodes + (owner * FACES + f) * HALO
            return table_ref.at[pl.ds(pl.multiple_of(at, HALO), HALO), :]

        table_ref[pl.ds(pl.multiple_of(e * size, size), size), :] = own
        node_copies = {}
        for t in (2, 1, 3, 0):
            who = (d, peer(t)) if t else (d, sib)
            node_copies[t] = send(node_at(e), node_at(e), node_sem, (t,), who)

        ids = lax.broadcasted_iota(jnp.int32, (size, HALO), 0)

        def picked(values, row):
            hit = jnp.where(ids == row, 1.0, 0.0).astype(BF16)
            return lax.dot_general(
                hit, values, (((0,), (0,)), ((), ())), preferred_element_type=F32
            ).astype(BF16)

        z_copies = {}
        for f in range(2):
            zface_ref[f] = picked(own, lists_ref[0, f : f + 1, :])
            for t in (2, 1, 3, 0):
                z_copies[f, t] = send(
                    zface_ref.at[f], halo_at(e, f), zf_sem, (f, t), (there[f], peer(t))
                )
        x_copies = {}
        forwards = []
        for t in range(chips):
            owner = source(t)
            if t:
                node_copies[t].wait_recv()
                forwards.append(send(node_at(owner), node_at(owner), fn_sem, (t,), (d, sib)))
                got_lists[t].wait_recv()
            values = node_ref_load(table_ref, owner, size)
            for f in range(2, 4):
                xface_ref[t, f - 2] = picked(values, lists_ref[t, f : f + 1, :])
                x_copies[f - 2, t] = send(
                    xface_ref.at[t, f - 2],
                    halo_at(owner, f),
                    xf_sem,
                    (f - 2, t),
                    (there[f], e),
                )
        for t in range(chips):
            for f in range(2):
                x_copies[f, t].wait_recv()
                place = halo_at(source(t), f + 2)
                forwards.append(send(place, place, fx_sem, (f, t), (d, sib)))
        for t in range(chips):
            for f in range(2):
                z_copies[f, t].wait_recv()
                place = halo_at(source(t), f)
                forwards.append(send(place, place, fz_sem, (f, t), (d, sib)))
        node_copies[0].wait_recv()
        for copy in forwards:
            copy.wait()
        for copy in got_lists[1:] + list(node_copies.values()):
            copy.wait_send()
        for copy in list(z_copies.values()) + list(x_copies.values()):
            copy.wait_send()
    for copy in sent:
        copy.wait_send()


def node_ref_load(table_ref, owner, size):
    return table_ref[pl.ds(pl.multiple_of(owner * size, size), size), :]


def node_step(own, reduce=None, lists=None, collective_id=0):
    vmem = pl.BlockSpec(memory_space=pltpu.VMEM)
    size, width = own.shape
    count = lax.axis_size("edge")
    chips = count // 2
    dma = pltpu.SemaphoreType.DMA
    args, outs, scratch = [own], [], []
    if reduce is not None:
        args += list(reduce)
        outs.append(jax.ShapeDtypeStruct(own.shape, BF16))
    if lists is not None:
        args.append(lists)
        rows = count * (size + FACES * HALO)
        outs.append(jax.ShapeDtypeStruct((rows, width), BF16))
    if reduce is not None:
        scratch += [pltpu.VMEM((chips, size, width), BF16)] * 3
        scratch += [dma((2, chips)), dma((2, chips))]
    if lists is not None:
        scratch += [
            pltpu.VMEM((chips, FACES, HALO), jnp.int32),
            pltpu.VMEM((2, HALO, width), BF16),
            pltpu.VMEM((chips, 2, HALO, width), BF16),
        ]
        scratch += [dma((2, chips)), dma((2, chips)), dma((2, 2, chips)), dma((2, 2, chips))]
        scratch += [dma((2, chips)), dma((2, 2, chips)), dma((2, 2, chips))]
    return pl.pallas_call(
        functools.partial(node_kernel, reduce is not None, lists is not None),
        out_shape=tuple(outs),
        in_specs=[vmem] * len(args),
        out_specs=(vmem,) * len(outs),
        scratch_shapes=scratch,
        compiler_params=pltpu.CompilerParams(
            collective_id=collective_id, has_side_effects=True, vmem_limit_bytes=48 * 2**20
        ),
        cost_estimate=pl.CostEstimate(flops=10**8, bytes_accessed=8 * 2**20, transcendentals=0),
        name="node_step",
    )(*args)


def shards(
    node_lat,
    edge_lat,
    senders,
    receivers,
    live_edges,
    send_rows,
    edge_w1,
    edge_b1,
    edge_w2,
    edge_gain,
    node_w1,
    node_b1,
    node_w2,
    node_gain,
):
    lists = send_rows[0]
    nodes = node_lat.shape[0] * lax.axis_size("edge")
    own, edges = node_lat, edge_lat
    (table,) = node_step(own, lists=lists, collective_id=0)
    for l in range(LAYERS):
        edges, part = edge_step(
            table,
            edges,
            senders,
            receivers,
            live_edges,
            edge_w1[l],
            edge_b1[l : l + 1],
            edge_w2[l],
            edge_gain[l : l + 1],
            nodes,
        )
        sums = (part, node_w1[l], node_b1[l : l + 1], node_w2[l], node_gain[l : l + 1])
        if l < LAYERS - 1:
            own, table = node_step(own, sums, lists, collective_id=1 + l)
        else:
            (own,) = node_step(own, sums, None, collective_id=1 + l)
    return (own, edges)


def solution(mesh):
    rows = P(("dom", "edge"), None)
    in_specs = (
        rows,
        rows,
        P(("dom", "edge")),
        P(("dom", "edge")),
        P("dom", "edge"),
        P(("dom", "edge"), None, None),
    ) + (P(),) * 8
    return jax.shard_map(
        shards, mesh=mesh, in_specs=in_specs, out_specs=(rows, rows), check_vma=False
    )
```

```python
import jax
import jax.numpy as jnp
from jax import lax
from jax.experimental import pallas as pl
from jax.experimental.pallas import tpu as pltpu
from jax.sharding import PartitionSpec as P

LAYERS = 2
EPS = 1e-05
FACES = 4
HALO = 128
GROUP = 64
CHUNK = 1536
STEP = 1024
MESH = pl.DeviceIdType.MESH
BF16 = jnp.bfloat16
F32 = jnp.float32
UP, DOWN, SIDE, ACROSS = range(4)
REACH = ({0, 1, 2, 3}, {1, 2, 3}, {3})


def dot(a, b):
    return jnp.dot(a, b, preferred_element_type=F32)


def layer_norm(values, gain):
    center = values - jnp.mean(values, axis=-1, keepdims=True)
    spread = jnp.mean(center * center, axis=-1, keepdims=True)
    return center * lax.rsqrt(spread + EPS) * gain


def rows(start, size):
    return pl.ds(pl.multiple_of(start, size), size)


def kernel(
    own_ref,
    edge_ref,
    send_ref,
    recv_ref,
    recv_row_ref,
    live_ref,
    list_ref,
    ew1_ref,
    eb1_ref,
    ew2_ref,
    eg_ref,
    nw1_ref,
    nb1_ref,
    nw2_ref,
    ng_ref,
    node_out_ref,
    edge_out_ref,
    table_ref,
    face_ref,
    lists_ref,
    mid_ref,
    s_ref,
    r_ref,
    pre_ref,
    msg_ref,
    part_ref,
    pair_ref,
    sums_ref,
    got_ref,
    block_send,
    block_recv,
    list_sem,
    pair_sem,
    sum_sem,
):
    d = lax.axis_index("dom")
    e = lax.axis_index("edge")
    doms = lax.axis_size("dom")
    count = lax.axis_size("edge")
    chips = count // 2
    last = chips - 1
    stride = doms // 4
    size, width = own_ref.shape
    half = width // 2
    edges = edge_ref.shape[0]
    nodes = count * size
    parts = size // HALO
    q = e // 2
    c = e % 2
    sib = (d, 2 * q + 1 - c)
    ups = (d, e + 2)
    downs = (d, e - 2)
    there = [(d + s) % doms for s in (1, doms - 1, stride, doms - stride)]

    def peer(t):
        return 2 * ((q + t) % chips) + c

    barrier = pltpu.get_barrier_semaphore()

    def greet(who):
        pl.semaphore_signal(barrier, inc=1, device_id=who, device_id_type=MESH)

    greet(sib)
    for t in range(1, chips):
        greet((d, peer(t)))
    for f in (2, 3):
        greet((there[f], e))
    for f in (0, 1):
        greet((there[f], 2 * (last - q) + c))
    pl.semaphore_wait(barrier, 1 + (chips - 1) + 2 + 2)

    lists_ref[pl.ds(q, 1)] = list_ref[...]
    for t in range(1, chips):
        pltpu.make_async_remote_copy(
            src_ref=list_ref,
            dst_ref=lists_ref.at[pl.ds(q, 1)],
            send_sem=list_sem.at[0, t],
            recv_sem=list_sem.at[1, t],
            device_id=(d, peer(t)),
            device_id_type=MESH,
        ).start()

    def list_copy(t):
        return pltpu.make_async_remote_copy(
            src_ref=list_ref,
            dst_ref=lists_ref.at[pl.ds((q + chips - t) % chips, 1)],
            send_sem=list_sem.at[0, t],
            recv_sem=list_sem.at[1, t],
            device_id=(d, peer(t)),
            device_id_type=MESH,
        )

    def exchange(l, own):
        def node_block(s, h, core=c):
            return (2 * s + core) * parts + h

        def halo_block(s, f, core=c):
            return count * parts + (2 * s + core) * FACES + f

        def block_at(block):
            return table_ref.at[l, rows(block * HALO, HALO), :]

        def copy(kind, block, who, src=None):
            return pltpu.make_async_remote_copy(
                src_ref=block_at(block) if src is None else src,
                dst_ref=block_at(block),
                send_sem=block_send.at[l, kind, block],
                recv_sem=block_recv.at[l, block],
                device_id=who,
                device_id_type=MESH,
            )

        sent = []

        def start(cond, kind, block, who, src=None):
            if cond is None:
                copy(kind, block, who, src).start()
            else:

                @pl.when(cond)
                def _():
                    copy(kind, block, who, src).start()

            return (kind, block, who, src)

        def wait(block):
            copy(SIDE, block, sib).wait_recv()

        ids = lax.broadcasted_iota(jnp.int32, (size, HALO), 0)

        def pick(s, f):
            hit = jnp.where(ids == lists_ref[s, f : f + 1, :], 1.0, 0.0).astype(BF16)
            values = table_ref[l, rows((2 * s + c) * size, size), :]
            face_ref[l, s, f] = lax.dot_general(
                hit, values, (((0,), (0,)), ((), ())), preferred_element_type=F32
            ).astype(BF16)

        def available(s):
            for edge_q, across in ((0, 2 * last + c), (last, c)):

                @pl.when((q == edge_q) & (s + edge_q != last if edge_q == 0 else s != 0))
                def _():
                    for f in (0, 1):
                        pick(s, f)
                        copy(
                            ACROSS, halo_block(s, f), (there[f], across), face_ref.at[l, s, f]
                        ).start()

            for f in (2, 3):
                pick(s, f)
                copy(ACROSS, halo_block(s, f), (there[f], e), face_ref.at[l, s, f]).start()

        table_ref[l, rows(e * size, size), :] = own
        for h in range(parts):
            start(q < last, UP, node_block(q, h), ups)
            start(q > 0, DOWN, node_block(q, h), downs)
        for h in range(parts):
            start(None, SIDE, node_block(q, h), sib)
        available(q)

        def from_line(s, onward, kind, who):
            for h in range(parts):
                block = node_block(s, h)
                wait(block)
                start(onward, kind, block, who)
                start(None, SIDE, block, sib)
            if l == 0:
                list_wait(s)
            available(s)

        def list_wait(s):
            for t in range(1, chips):

                @pl.when((q + chips - s) % chips == t)
                def _():
                    list_copy(t).wait_recv()

        def from_x(s):
            for f in (2, 3):
                block = halo_block(s, f)
                wait(block)
                start(None, SIDE, block, sib)

        def from_z(s, onward, kind, who):
            for f in (0, 1):
                block = halo_block(s, f)
                wait(block)
                if onward:
                    start(None, kind, block, who)
                start(None, SIDE, block, sib)

        for k in range(1, chips + 1):
            for flow, (kind, who) in enumerate(((DOWN, downs), (UP, ups))):
                for a, reach in enumerate(REACH):
                    place = chips + a - k
                    if place not in reach:
                        continue
                    s = last - a if flow else a
                    at = last - place if flow else place
                    onward = place - 1 in reach

                    @pl.when(q == at)
                    def _():
                        from_z(s, onward, kind, who)

            if k < chips:

                @pl.when(q >= k)
                def _():
                    from_line(q - k, q < last, UP, ups)

                @pl.when(q + k <= last)
                def _():
                    from_line(q + k, q > 0, DOWN, downs)

            if k == 1:
                from_x(q)
            else:

                @pl.when(q >= k - 1)
                def _():
                    from_x(q - (k - 1))

                @pl.when(q + k - 1 <= last)
                def _():
                    from_x(q + k - 1)

        def finish_nodes():
            for s in range(chips):
                for h in range(parts):
                    wait(node_block(s, h, 1 - c))

        def finish_halo():
            for s in range(chips):
                for f in range(FACES):
                    wait(halo_block(s, f, 1 - c))

        def finish_sends():
            for s in range(chips):
                for h in range(parts):
                    block = node_block(s, h)
                    pl.when((q < last) & (s <= q))(lambda: copy(UP, block, ups).wait_send())
                    pl.when((q > 0) & (s >= q))(lambda: copy(DOWN, block, downs).wait_send())
                    copy(SIDE, block, sib).wait_send()
                for f in range(FACES):
                    block = halo_block(s, f)
                    copy(SIDE, block, sib).wait_send()
                    if f >= 2:
                        copy(ACROSS, block, sib, face_ref.at[l, s, f]).wait_send()
                    else:
                        cond = (q == 0) if s != last else None
                        if s != 0:
                            cond = (q == last) if cond is None else cond | (q == last)
                        pl.when(cond)(
                            lambda: copy(ACROSS, block, sib, face_ref.at[l, s, f]).wait_send()
                        )
                        if s < len(REACH):
                            for place in REACH[s]:
                                if place - 1 in REACH[s]:
                                    pl.when(q == place)(
                                        lambda: copy(DOWN, block, downs).wait_send()
                                    )
                        if last - s < len(REACH):
                            for place in REACH[last - s]:
                                if place - 1 in REACH[last - s]:
                                    pl.when(q == last - place)(
                                        lambda: copy(UP, block, ups).wait_send()
                                    )

        return finish_nodes, finish_halo, finish_sends

    def project(l, out_ref, part, first, stop, bias):
        for base in range(first, stop, STEP):
            val = dot(
                table_ref[l, base : base + STEP, :],
                ew1_ref[l, part * width : (part + 1) * width, :],
            )
            if bias is not None:
                val = val + bias
            out_ref[pl.ds(base, STEP), 0, :] = val[:, :half]
            out_ref[pl.ds(base, STEP), 1, :] = val[:, half:]

    def edge_phase(l, in_ref, out_ref):
        @pl.loop(0, edges // GROUP)
        def _(g):
            for u in range(GROUP):
                k = g * GROUP + u
                a = send_ref[k]
                b = recv_ref[k]
                at = pl.multiple_of(g * (2 * GROUP), 2 * GROUP) + 2 * u
                pre_ref[pl.ds(at, 2), :] = s_ref[a] + r_ref[b]

        live = live_ref[0, 0]

        @pl.loop(0, edges // CHUNK)
        def _(i):
            base = pl.multiple_of(i * CHUNK, CHUNK)
            old = in_ref[pl.ds(base, CHUNK), :]
            pre = dot(old, ew1_ref[l, :width, :])
            low = pre[:, :half] + pre_ref[pl.ds(2 * base, CHUNK, stride=2), :]
            high = pre[:, half:] + pre_ref[pl.ds(2 * base + 1, CHUNK, stride=2), :]
            hidden = jnp.maximum(jnp.concatenate([low, high], axis=1), 0.0).astype(BF16)
            message = layer_norm(dot(hidden, ew2_ref[l]), eg_ref[l : l + 1, :])
            slot = lax.broadcasted_iota(jnp.int32, (CHUNK, 1), 0) + base
            message = jnp.where(slot < live, message, 0.0)
            out_ref[pl.ds(base, CHUNK), :] = (old.astype(F32) + message).astype(BF16)
            msg_ref[pl.ds(base, CHUNK), :] = message.astype(BF16)

    def scatter(owner):
        depth = 512
        ids = lax.broadcasted_iota(jnp.int32, (size, depth), 0) + owner * size
        acc = jnp.zeros((size, width), F32)
        for j in range(0, edges, depth):
            hit = ids == recv_row_ref[:, j : j + depth]
            acc = acc + dot(jnp.where(hit, 1.0, 0.0).astype(BF16), msg_ref[j : j + depth, :])
        return acc

    def reduce_phase(l, own):
        def pair_copy(t):
            return pltpu.make_async_remote_copy(
                src_ref=part_ref.at[l, t],
                dst_ref=pair_ref.at[l, t],
                send_sem=pair_sem.at[l, 0, t],
                recv_sem=pair_sem.at[l, 1, t],
                device_id=sib,
                device_id_type=MESH,
            )

        def sum_copy(t):
            return pltpu.make_async_remote_copy(
                src_ref=sums_ref.at[l, t],
                dst_ref=got_ref.at[l, t],
                send_sem=sum_sem.at[l, 0, t],
                recv_sem=sum_sem.at[l, 1, t],
                device_id=(d, peer(t)),
                device_id_type=MESH,
            )

        order = (2, 3, 1, 0)
        for t in order:
            part_ref[l, t] = scatter(2 * ((q + t) % chips) + 1 - c).astype(BF16)
            pair_copy(t).start()
        mine = None
        for t in order:
            total = scatter(peer(t))
            pair_copy(t).wait_recv()
            total = total + pair_ref[l, t].astype(F32)
            if t:
                sums_ref[l, t] = total.astype(BF16)
                sum_copy(t).start()
            else:
                mine = total
        pre = dot(own, nw1_ref[l, :width, :]) + nb1_ref[l : l + 1, :]
        for t in order[:-1]:
            sum_copy(t).wait_recv()
            mine = mine + got_ref[l, t].astype(F32)
        pre = pre + dot(mine.astype(BF16), nw1_ref[l, width:, :])
        hidden = jnp.maximum(pre, 0.0).astype(BF16)
        update = layer_norm(dot(hidden, nw2_ref[l]), ng_ref[l : l + 1, :])
        new = (own.astype(F32) + update).astype(BF16)

        def finish_sends():
            for t in order:
                pair_copy(t).wait_send()
                if t:
                    sum_copy(t).wait_send()

        return new, finish_sends

    own = own_ref[...]
    pending = []
    for l in range(LAYERS):
        finish_nodes, finish_halo, finish_sends = exchange(l, own)
        pending.append(finish_sends)
        finish_nodes()
        project(l, s_ref, 1, 0, nodes, None)
        project(l, r_ref, 2, 0, nodes, eb1_ref[l : l + 1, :])
        finish_halo()
        project(l, s_ref, 1, nodes, table_ref.shape[1], None)
        edge_phase(l, edge_ref if l == 0 else mid_ref, edge_out_ref if l == LAYERS - 1 else mid_ref)
        own, finish_sums = reduce_phase(l, own)
        pending.append(finish_sums)
    node_out_ref[...] = own
    for finish in pending:
        finish()
    for t in range(1, chips):
        list_copy(t).wait_send()


def shards(
    node_lat,
    edge_lat,
    senders,
    receivers,
    live_edges,
    send_rows,
    edge_w1,
    edge_b1,
    edge_w2,
    edge_gain,
    node_w1,
    node_b1,
    node_w2,
    node_gain,
):
    vmem = pl.BlockSpec(memory_space=pltpu.VMEM)
    smem = pl.BlockSpec(memory_space=pltpu.SMEM)
    dma = pltpu.SemaphoreType.DMA
    size, width = node_lat.shape
    edges = edge_lat.shape[0]
    count = lax.axis_size("edge")
    chips = count // 2
    nodes = count * size
    table = count * (size + FACES * HALO)
    blocks = table // HALO
    half = width // 2
    sums = pltpu.VMEM((LAYERS, chips, size, width), BF16)
    return pl.pallas_call(
        kernel,
        out_shape=(
            jax.ShapeDtypeStruct(node_lat.shape, BF16),
            jax.ShapeDtypeStruct(edge_lat.shape, BF16),
        ),
        in_specs=[vmem, vmem, smem, smem, vmem, smem] + [vmem] * 9,
        out_specs=(vmem, vmem),
        scratch_shapes=[
            pltpu.VMEM((LAYERS, table, width), BF16),
            pltpu.VMEM((LAYERS, chips, FACES, HALO, width), BF16),
            pltpu.VMEM((chips, FACES, HALO), jnp.int32),
            pltpu.VMEM((edges, width), BF16),
            pltpu.VMEM((table, 2, half), F32),
            pltpu.VMEM((nodes, 2, half), F32),
            pltpu.VMEM((2 * edges, half), F32),
            pltpu.VMEM((edges, width), BF16),
            sums,
            sums,
            sums,
            sums,
            dma((LAYERS, 4, blocks)),
            dma((LAYERS, blocks)),
            dma((2, chips)),
            dma((LAYERS, 2, chips)),
            dma((LAYERS, 2, chips)),
        ],
        compiler_params=pltpu.CompilerParams(
            collective_id=0, has_side_effects=True, vmem_limit_bytes=56 * 2**20
        ),
        cost_estimate=pl.CostEstimate(
            flops=2 * 10**10, bytes_accessed=8 * 2**20, transcendentals=0
        ),
        name="graph_layers",
    )(
        node_lat,
        edge_lat,
        senders,
        receivers,
        receivers.reshape(1, -1),
        live_edges,
        send_rows,
        edge_w1,
        edge_b1,
        edge_w2,
        edge_gain,
        node_w1,
        node_b1,
        node_w2,
        node_gain,
    )


def solution(mesh):
    split = P(("dom", "edge"), None)
    in_specs = (
        split,
        split,
        P(("dom", "edge")),
        P(("dom", "edge")),
        P("dom", "edge"),
        P(("dom", "edge"), None, None),
    ) + (P(),) * 8
    return jax.shard_map(
        shards, mesh=mesh, in_specs=in_specs, out_specs=(split, split), check_vma=False
    )
```

```python
import jax
import jax.numpy as jnp
from jax import lax
from jax.experimental import pallas as pl
from jax.experimental.pallas import tpu as pltpu
from jax.sharding import PartitionSpec as P

LAYERS = 2
EPS = 1e-05
FACES = 4
HALO = 128
GROUP = 32
CHUNK = 1024
STEP = 1024
MESH = pl.DeviceIdType.MESH
BF16 = jnp.bfloat16
F32 = jnp.float32
UP, DOWN, SIDE, ACROSS = range(4)
REACH = (0, 1, 3)


def dot(a, b):
    return jnp.dot(a, b, preferred_element_type=F32)


def layer_norm(values, gain):
    center = values - jnp.mean(values, axis=-1, keepdims=True)
    spread = jnp.mean(center * center, axis=-1, keepdims=True)
    return center * lax.rsqrt(spread + EPS) * gain


def rows(start, size):
    return pl.ds(pl.multiple_of(start, size), size)


def kernel(
    own_ref,
    edge_ref,
    send_ref,
    recv_ref,
    recv_row_ref,
    live_ref,
    list_ref,
    ew1_ref,
    eb1_ref,
    ew2_ref,
    eg_ref,
    nw1_ref,
    nb1_ref,
    nw2_ref,
    ng_ref,
    node_out_ref,
    edge_out_ref,
    table_ref,
    face_ref,
    lists_ref,
    mid_ref,
    s_ref,
    r_ref,
    pre_ref,
    msg_ref,
    part_ref,
    pair_ref,
    sums_ref,
    got_ref,
    sum_ref,
    node_ref,
    block_send,
    block_recv,
    list_sem,
    pair_sem,
    sum_sem,
    local_sem,
):
    d = lax.axis_index("dom")
    e = lax.axis_index("edge")
    doms = lax.axis_size("dom")
    count = lax.axis_size("edge")
    chips = count // 2
    last = chips - 1
    stride = doms // 4
    size, width = own_ref.shape
    half = width // 2
    edges = edge_ref.shape[0]
    nodes = count * size
    parts = size // HALO
    q = e // 2
    c = e % 2
    sib = (d, 2 * q + 1 - c)
    ups = (d, e + 2)
    downs = (d, e - 2)
    there = [(d + s) % doms for s in (1, doms - 1, stride, doms - stride)]

    def peer(t):
        return 2 * ((q + t) % chips) + c

    barrier = pltpu.get_barrier_semaphore()

    def greet(who):
        pl.semaphore_signal(barrier, inc=1, device_id=who, device_id_type=MESH)

    greet(sib)
    for t in range(1, chips):
        greet((d, peer(t)))
    for f in (2, 3):
        greet((there[f], e))
    for f in (0, 1):
        greet((there[f], 2 * (last - q) + c))
    pl.semaphore_wait(barrier, 1 + (chips - 1) + 2 + 2)

    def edge_load():
        return pltpu.make_async_copy(edge_ref, mid_ref, local_sem.at[0])

    def edge_store():
        return pltpu.make_async_copy(mid_ref, edge_out_ref, local_sem.at[1])

    def list_copy(t):
        return pltpu.make_async_remote_copy(
            src_ref=list_ref,
            dst_ref=lists_ref.at[pl.ds(q, 1)],
            send_sem=list_sem.at[0, t],
            recv_sem=list_sem.at[1, t],
            device_id=(d, peer(t)),
            device_id_type=MESH,
        )

    edge_load().start()
    lists_ref[pl.ds(q, 1)] = list_ref[...]
    for t in range(1, chips):
        list_copy(t).start()
    node_ref[...] = own_ref[...]

    def exchange(l):
        def node_block(s, h, core=c):
            return (2 * s + core) * parts + h

        def halo_block(s, f, core=c):
            return count * parts + (2 * s + core) * FACES + f

        def block_at(block):
            return table_ref.at[l, rows(block * HALO, HALO), :]

        def copy(kind, block, who, src=None):
            return pltpu.make_async_remote_copy(
                src_ref=block_at(block) if src is None else src,
                dst_ref=block_at(block),
                send_sem=block_send.at[l, kind, block],
                recv_sem=block_recv.at[l, block],
                device_id=who,
                device_id_type=MESH,
            )

        def start(cond, kind, block, who):
            if cond is None:
                copy(kind, block, who).start()
            else:
                pl.when(cond)(lambda: copy(kind, block, who).start())

        def wait(block):
            copy(SIDE, block, sib).wait_recv()

        ids = lax.broadcasted_iota(jnp.int32, (size, HALO), 0)

        def pick(s, f, who):
            hit = jnp.where(ids == lists_ref[s, pl.ds(f, 1), :], 1.0, 0.0).astype(BF16)
            values = table_ref[l, rows((2 * s + c) * size, size), :]
            face_ref[l, s, f] = lax.dot_general(
                hit, values, (((0,), (0,)), ((), ())), preferred_element_type=F32
            ).astype(BF16)
            copy(ACROSS, halo_block(s, f), who, face_ref.at[l, s, f]).start()

        def at_end(s):
            return ((q == 0) & (s != last)) | ((q == last) & (s != 0))

        def available(s):
            @pl.when(at_end(s))
            def _():
                @pl.loop(0, 2)
                def _(f):
                    pick(s, f, ((d + doms + 1 - 2 * f) % doms, 2 * (last - q) + c))

            @pl.loop(2, FACES)
            def _(f):
                pick(s, f, ((d + doms + stride * (5 - 2 * f)) % doms, e))

        table_ref[l, rows(e * size, size), :] = node_ref[...]
        for h in range(parts):
            start(q < last, UP, node_block(q, h), ups)
            start(q > 0, DOWN, node_block(q, h), downs)
        for h in range(parts):
            start(None, SIDE, node_block(q, h), sib)
        available(q)

        def from_line(s, onward, kind, who):
            for h in range(parts):
                block = node_block(s, h)
                wait(block)
                start(onward, kind, block, who)
                start(None, SIDE, block, sib)

            @pl.when(l == 0)
            def _():
                list_copy((q + chips - s) % chips).wait_recv()

            available(s)

        def from_x(s):
            for f in (2, 3):
                block = halo_block(s, f)
                wait(block)
                start(None, SIDE, block, sib)

        def from_z(s, onward, kind, who):
            for f in (0, 1):
                block = halo_block(s, f)
                wait(block)
                start(onward, kind, block, who)
                start(None, SIDE, block, sib)

        @pl.loop(1, chips + 1)
        def _(k):
            for kind, who in ((DOWN, downs), (UP, ups)):
                for a, least in enumerate(REACH):
                    place = chips + a - k
                    mine = q if kind == DOWN else last - q
                    s = a if kind == DOWN else last - a

                    @pl.when((mine == place) & (place >= least))
                    def _():
                        from_z(s, place > least, kind, who)

            @pl.when((k < chips) & (q >= k))
            def _():
                from_line(q - k, q < last, UP, ups)

            @pl.when((k < chips) & (q + k <= last))
            def _():
                from_line(q + k, q > 0, DOWN, downs)

            @pl.when(q >= k - 1)
            def _():
                from_x(q - (k - 1))

            @pl.when((k > 1) & (q + k - 1 <= last))
            def _():
                from_x(q + k - 1)

        def finish_nodes():
            @pl.loop(0, chips)
            def _(s):
                for h in range(parts):
                    wait(node_block(s, h, 1 - c))

        def finish_halo():
            @pl.loop(0, chips)
            def _(s):
                for f in range(FACES):
                    wait(halo_block(s, f, 1 - c))

        def finish_sends():
            for s in range(chips):
                low = REACH[s] if s < last else chips
                high = REACH[last - s] if s else chips
                for h in range(parts):
                    block = node_block(s, h)
                    pl.when((q < last) & (s <= q))(lambda: copy(UP, block, ups).wait_send())
                    pl.when((q > 0) & (s >= q))(lambda: copy(DOWN, block, downs).wait_send())
                    copy(SIDE, block, sib).wait_send()
                for f in range(FACES):
                    block = halo_block(s, f)
                    across = copy(ACROSS, block, sib, face_ref.at[l, s, f])
                    copy(SIDE, block, sib).wait_send()
                    if f >= 2:
                        across.wait_send()
                    else:
                        pl.when(at_end(s))(across.wait_send)
                        pl.when(q > low)(lambda: copy(DOWN, block, downs).wait_send())
                        pl.when(last - q > high)(lambda: copy(UP, block, ups).wait_send())

        return finish_nodes, finish_halo, finish_sends

    def project(l, out_ref, part, first, stop, bias):
        @pl.loop(first // STEP, stop // STEP)
        def _(i):
            base = pl.multiple_of(i * STEP, STEP)
            val = dot(
                table_ref[l, pl.ds(base, STEP), :],
                ew1_ref[l, part * width : (part + 1) * width, :],
            )
            if bias is not None:
                val = val + bias
            out_ref[pl.ds(2 * base, STEP, stride=2), :] = val[:, :half]
            out_ref[pl.ds(2 * base + 1, STEP, stride=2), :] = val[:, half:]

    def edge_phase(l):
        @pl.loop(0, edges // GROUP)
        def _(g):
            for u in range(GROUP):
                k = g * GROUP + u
                a = send_ref[k]
                b = recv_ref[k]
                at = pl.multiple_of(g * (2 * GROUP), 2 * GROUP) + 2 * u
                pre_ref[pl.ds(at, 2), :] = s_ref[pl.ds(2 * a, 2), :] + r_ref[pl.ds(2 * b, 2), :]

        pl.when(l == 0)(lambda: edge_load().wait())
        live = live_ref[0, 0]

        @pl.loop(0, edges // CHUNK)
        def _(i):
            base = pl.multiple_of(i * CHUNK, CHUNK)
            old = mid_ref[pl.ds(base, CHUNK), :]
            pre = dot(old, ew1_ref[l, :width, :])
            low = pre[:, :half] + pre_ref[pl.ds(2 * base, CHUNK, stride=2), :]
            high = pre[:, half:] + pre_ref[pl.ds(2 * base + 1, CHUNK, stride=2), :]
            hidden = jnp.maximum(jnp.concatenate([low, high], axis=1), 0.0).astype(BF16)
            message = layer_norm(dot(hidden, ew2_ref[l]), eg_ref[pl.ds(l, 1), :])
            slot = lax.broadcasted_iota(jnp.int32, (CHUNK, 1), 0) + base
            message = jnp.where(slot < live, message, 0.0)
            mid_ref[pl.ds(base, CHUNK), :] = (old.astype(F32) + message).astype(BF16)
            msg_ref[pl.ds(base, CHUNK), :] = message.astype(BF16)

        pl.when(l == LAYERS - 1)(lambda: edge_store().start())

    def scatter(owner):
        depth = 512
        ids = lax.broadcasted_iota(jnp.int32, (size, depth), 0) + owner * size
        acc = jnp.zeros((size, width), F32)
        for j in range(0, edges, depth):
            hit = ids == recv_row_ref[:, j : j + depth]
            acc = acc + dot(jnp.where(hit, 1.0, 0.0).astype(BF16), msg_ref[j : j + depth, :])
        return acc

    def reduce_phase(l):
        def pair_copy(t):
            return pltpu.make_async_remote_copy(
                src_ref=part_ref.at[l, t],
                dst_ref=pair_ref.at[l, t],
                send_sem=pair_sem.at[l, 0, t],
                recv_sem=pair_sem.at[l, 1, t],
                device_id=sib,
                device_id_type=MESH,
            )

        def sum_copy(t):
            return pltpu.make_async_remote_copy(
                src_ref=sums_ref.at[l, t],
                dst_ref=got_ref.at[l, t],
                send_sem=sum_sem.at[l, 0, t],
                recv_sem=sum_sem.at[l, 1, t],
                device_id=(d, peer(t)),
                device_id_type=MESH,
            )

        @pl.loop(1, chips + 1)
        def _(i):
            t = i % chips
            part_ref[l, t] = scatter(2 * ((q + t) % chips) + 1 - c).astype(BF16)
            pair_copy(t).start()

        @pl.loop(1, chips + 1)
        def _(i):
            t = i % chips
            total = scatter(peer(t))
            pair_copy(t).wait_recv()
            total = total + pair_ref[l, t].astype(F32)
            sum_ref[...] = total
            sums_ref[l, t] = total.astype(BF16)
            pl.when(t > 0)(lambda: sum_copy(t).start())

        own = node_ref[...]
        mine = sum_ref[...]
        pre = dot(own, nw1_ref[l, :width, :]) + nb1_ref[pl.ds(l, 1), :]
        for t in range(1, chips):
            sum_copy(t).wait_recv()
            mine = mine + got_ref[l, t].astype(F32)
        pre = pre + dot(mine.astype(BF16), nw1_ref[l, width:, :])
        hidden = jnp.maximum(pre, 0.0).astype(BF16)
        update = layer_norm(dot(hidden, nw2_ref[l]), ng_ref[pl.ds(l, 1), :])
        node_ref[...] = (own.astype(F32) + update).astype(BF16)
        for t in range(chips):
            pair_copy(t).wait_send()
            if t:
                sum_copy(t).wait_send()

    @pl.loop(0, LAYERS)
    def _(l):
        finish_nodes, finish_halo, finish_sends = exchange(l)
        finish_nodes()
        project(l, s_ref, 1, 0, nodes, None)
        project(l, r_ref, 2, 0, nodes, eb1_ref[pl.ds(l, 1), :])
        finish_halo()
        project(l, s_ref, 1, nodes, table_ref.shape[1], None)
        edge_phase(l)
        finish_sends()
        reduce_phase(l)

    node_out_ref[...] = node_ref[...]
    edge_store().wait()
    for t in range(1, chips):
        list_copy(t).wait_send()


def settle_kernel(node_ref, edge_ref, node_out_ref, edge_out_ref, node_buf, edge_buf, sems):
    pieces = 4
    size = edge_ref.shape[0] // pieces
    moves = [(node_ref, node_buf, node_out_ref)]
    for i in range(pieces):
        part = pl.ds(i * size, size)
        moves.append((edge_ref.at[part], edge_buf.at[part], edge_out_ref.at[part]))
    loads = [
        pltpu.make_async_copy(move[0], move[1], sems.at[0, i]) for i, move in enumerate(moves)
    ]
    stores = [
        pltpu.make_async_copy(move[1], move[2], sems.at[1, i]) for i, move in enumerate(moves)
    ]
    for load in loads:
        load.start()
    for load, store in zip(loads, stores):
        load.wait()
        store.start()
    for store in stores:
        store.wait()


def shards(
    node_lat,
    edge_lat,
    senders,
    receivers,
    live_edges,
    send_rows,
    edge_w1,
    edge_b1,
    edge_w2,
    edge_gain,
    node_w1,
    node_b1,
    node_w2,
    node_gain,
):
    vmem = pl.BlockSpec(memory_space=pltpu.VMEM)
    smem = pl.BlockSpec(memory_space=pltpu.SMEM)
    hbm = pl.BlockSpec(memory_space=pl.ANY)
    dma = pltpu.SemaphoreType.DMA
    size, width = node_lat.shape
    edges = edge_lat.shape[0]
    count = lax.axis_size("edge")
    chips = count // 2
    nodes = count * size
    table = count * (size + FACES * HALO)
    blocks = table // HALO
    half = width // 2
    sums = pltpu.VMEM((LAYERS, chips, size, width), BF16)
    outs = (
        jax.ShapeDtypeStruct(node_lat.shape, BF16),
        jax.ShapeDtypeStruct(edge_lat.shape, BF16),
    )
    own, moved = pl.pallas_call(
        kernel,
        out_shape=outs,
        in_specs=[vmem, hbm, smem, smem, vmem, smem] + [vmem] * 9,
        out_specs=(vmem, hbm),
        scratch_shapes=[
            pltpu.VMEM((LAYERS, table, width), BF16),
            pltpu.VMEM((LAYERS, chips, FACES, HALO, width), BF16),
            pltpu.VMEM((chips, FACES, HALO), jnp.int32),
            pltpu.VMEM((edges, width), BF16),
            pltpu.VMEM((2 * table, half), F32),
            pltpu.VMEM((2 * nodes, half), F32),
            pltpu.VMEM((2 * edges, half), F32),
            pltpu.VMEM((edges, width), BF16),
            sums,
            sums,
            sums,
            sums,
            pltpu.VMEM((size, width), F32),
            pltpu.VMEM((size, width), BF16),
            dma((LAYERS, 4, blocks)),
            dma((LAYERS, blocks)),
            dma((2, chips)),
            dma((LAYERS, 2, chips)),
            dma((LAYERS, 2, chips)),
            dma((2,)),
        ],
        compiler_params=pltpu.CompilerParams(
            collective_id=0, has_side_effects=True, vmem_limit_bytes=56 * 2**20
        ),
        cost_estimate=pl.CostEstimate(
            flops=2 * 10**10, bytes_accessed=8 * 2**20, transcendentals=0
        ),
        name="graph_layers",
    )(
        node_lat,
        edge_lat,
        senders,
        receivers,
        receivers.reshape(1, -1),
        live_edges,
        send_rows,
        edge_w1,
        edge_b1,
        edge_w2,
        edge_gain,
        node_w1,
        node_b1,
        node_w2,
        node_gain,
    )
    return pl.pallas_call(
        settle_kernel,
        out_shape=outs,
        in_specs=[hbm, hbm],
        out_specs=(hbm, hbm),
        scratch_shapes=[
            pltpu.VMEM(node_lat.shape, BF16),
            pltpu.VMEM(edge_lat.shape, BF16),
            dma((2, 5)),
        ],
        name="settle",
    )(own, moved)


def solution(mesh):
    split = P(("dom", "edge"), None)
    in_specs = (
        split,
        split,
        P(("dom", "edge")),
        P(("dom", "edge")),
        P("dom", "edge"),
        P(("dom", "edge"), None, None),
    ) + (P(),) * 8
    return jax.shard_map(
        shards, mesh=mesh, in_specs=in_specs, out_specs=(split, split), check_vma=False
    )
```

```python
import jax
import jax.numpy as jnp
from jax import lax
from jax.experimental import pallas as pl
from jax.experimental.pallas import tpu as pltpu
from jax.sharding import PartitionSpec as P

LAYERS = 2
EPS = 1e-05
FACES = 4
HALO = 128
GROUP = 32
CHUNK = 1024
STEP = 1024
MESH = pl.DeviceIdType.MESH
BF16 = jnp.bfloat16
F32 = jnp.float32
UP, DOWN, SIDE, ACROSS, BEYOND = range(5)
REACH = (0, 1, 3)


def dot(a, b):
    return jnp.dot(a, b, preferred_element_type=F32)


def layer_norm(values, gain):
    center = values - jnp.mean(values, axis=-1, keepdims=True)
    spread = jnp.mean(center * center, axis=-1, keepdims=True)
    return center * lax.rsqrt(spread + EPS) * gain


def rows(start, size):
    return pl.ds(pl.multiple_of(start, size), size)


def kernel(
    own_ref,
    edge_ref,
    send_ref,
    recv_ref,
    live_ref,
    list_ref,
    recv_row_hbm,
    ew1_hbm,
    eb1_hbm,
    ew2_hbm,
    eg_hbm,
    nw1_hbm,
    nb1_hbm,
    nw2_hbm,
    ng_hbm,
    node_out_ref,
    edge_out_ref,
    recv_row_ref,
    ew1_ref,
    eb1_ref,
    ew2_ref,
    eg_ref,
    nw1_ref,
    nb1_ref,
    nw2_ref,
    ng_ref,
    table_ref,
    face_ref,
    lists_ref,
    mid_ref,
    s_ref,
    r_ref,
    pre_ref,
    msg_ref,
    part_ref,
    pair_ref,
    sums_ref,
    got_ref,
    sum_ref,
    node_ref,
    block_send,
    block_recv,
    list_sem,
    pair_sem,
    sum_sem,
    local_sem,
    load_sem,
):
    d = lax.axis_index("dom")
    e = lax.axis_index("edge")
    doms = lax.axis_size("dom")
    count = lax.axis_size("edge")
    chips = count // 2
    last = chips - 1
    stride = doms // 4
    size, width = own_ref.shape
    half = width // 2
    edges = edge_ref.shape[0]
    nodes = count * size
    parts = size // HALO
    q = e // 2
    c = e % 2
    sib = (d, 2 * q + 1 - c)
    beside = q + 1 - 2 * (q % 2)
    ups = (d, e + 2)
    downs = (d, e - 2)
    there = [(d + s) % doms for s in (1, doms - 1, stride, doms - stride)]

    def peer(t):
        return 2 * ((q + t) % chips) + c

    def loads():
        pairs = (
            (ew1_hbm, ew1_ref),
            (eb1_hbm, eb1_ref),
            (ew2_hbm, ew2_ref),
            (eg_hbm, eg_ref),
            (recv_row_hbm, recv_row_ref),
            (nw1_hbm, nw1_ref),
            (nb1_hbm, nb1_ref),
            (nw2_hbm, nw2_ref),
            (ng_hbm, ng_ref),
        )
        return [
            pltpu.make_async_copy(src, dst, load_sem.at[i]) for i, (src, dst) in enumerate(pairs)
        ]

    def edge_load():
        return pltpu.make_async_copy(edge_ref, mid_ref, local_sem.at[0])

    for load in loads():
        load.start()
    edge_load().start()

    barrier = pltpu.get_barrier_semaphore()

    def greet(who):
        pl.semaphore_signal(barrier, inc=1, device_id=who, device_id_type=MESH)

    greet(sib)
    for t in range(1, chips):
        greet((d, peer(t)))
    for f in (2, 3):
        greet((there[f], e))
    for f in (0, 1):
        greet((there[f], 2 * (last - q) + c))
        greet((there[f], 2 * beside + c))
    pl.semaphore_wait(barrier, 1 + (chips - 1) + 2 + 2 + 2)

    def edge_store():
        return pltpu.make_async_copy(mid_ref, edge_out_ref, local_sem.at[1])

    def list_copy(t):
        return pltpu.make_async_remote_copy(
            src_ref=list_ref,
            dst_ref=lists_ref.at[pl.ds(q, 1)],
            send_sem=list_sem.at[0, t],
            recv_sem=list_sem.at[1, t],
            device_id=(d, peer(t)),
            device_id_type=MESH,
        )

    lists_ref[pl.ds(q, 1)] = list_ref[...]
    for t in range(1, chips):
        list_copy(t).start()
    node_ref[...] = own_ref[...]

    def exchange(l):
        def node_block(s, h, core=c):
            return (2 * s + core) * parts + h

        def halo_block(s, f, core=c):
            return count * parts + (2 * s + core) * FACES + f

        def block_at(block):
            return table_ref.at[l, rows(block * HALO, HALO), :]

        def copy(kind, block, who, src=None):
            return pltpu.make_async_remote_copy(
                src_ref=block_at(block) if src is None else src,
                dst_ref=block_at(block),
                send_sem=block_send.at[l, kind, block],
                recv_sem=block_recv.at[l, block],
                device_id=who,
                device_id_type=MESH,
            )

        def start(cond, kind, block, who):
            if cond is None:
                copy(kind, block, who).start()
            else:
                pl.when(cond)(lambda: copy(kind, block, who).start())

        def wait(block):
            copy(SIDE, block, sib).wait_recv()

        ids = lax.broadcasted_iota(jnp.int32, (size, HALO), 0)

        def pick(s, f, who):
            hit = jnp.where(ids == lists_ref[s, pl.ds(f, 1), :], 1.0, 0.0).astype(BF16)
            values = table_ref[l, rows((2 * s + c) * size, size), :]
            face_ref[l, s, f] = lax.dot_general(
                hit, values, (((0,), (0,)), ((), ())), preferred_element_type=F32
            ).astype(BF16)
            copy(ACROSS, halo_block(s, f), who, face_ref.at[l, s, f]).start()

        def at_end(s):
            return ((q == 0) & (s != last)) | ((q == last) & (s != 0))

        def twice(s):
            return ((q == 0) & (s < last - 1)) | ((q == last) & (s > 1))

        def available(s):
            @pl.when(at_end(s))
            def _():
                @pl.loop(0, 2)
                def _(f):
                    dom = (d + doms + 1 - 2 * f) % doms
                    pick(s, f, (dom, 2 * (last - q) + c))

                    @pl.when(twice(s))
                    def _():
                        copy(
                            BEYOND, halo_block(s, f), (dom, 2 * beside + c), face_ref.at[l, s, f]
                        ).start()

            @pl.loop(2, FACES)
            def _(f):
                pick(s, f, ((d + doms + stride * (5 - 2 * f)) % doms, e))

        table_ref[l, rows(e * size, size), :] = node_ref[...]
        for h in range(parts):
            start(q < last, UP, node_block(q, h), ups)
            start(q > 0, DOWN, node_block(q, h), downs)
        for h in range(parts):
            start(None, SIDE, node_block(q, h), sib)
        available(q)

        def from_line(s, onward, kind, who):
            for h in range(parts):
                block = node_block(s, h)
                wait(block)
                start(onward, kind, block, who)
                start(None, SIDE, block, sib)

            @pl.when(l == 0)
            def _():
                list_copy((q + chips - s) % chips).wait_recv()

            available(s)

        def from_x(s):
            for f in (2, 3):
                block = halo_block(s, f)
                wait(block)
                start(None, SIDE, block, sib)

        def from_z(s, onward, kind, who):
            for f in (0, 1):
                block = halo_block(s, f)
                wait(block)
                start(onward, kind, block, who)
                start(None, SIDE, block, sib)

        @pl.loop(1, chips + 1)
        def _(k):
            for kind, who in ((DOWN, downs), (UP, ups)):
                for a, least in enumerate(REACH):
                    mine = q if kind == DOWN else last - q
                    s = a if kind == DOWN else last - a
                    entry = mine % 2 == 1

                    @pl.when((k == 2 + a - mine % 2) & (mine >= least))
                    def _():
                        from_z(s, entry & (mine > least), kind, who)

            @pl.when((k < chips) & (q >= k))
            def _():
                from_line(q - k, q < last, UP, ups)

            @pl.when((k < chips) & (q + k <= last))
            def _():
                from_line(q + k, q > 0, DOWN, downs)

            @pl.when(q >= k - 1)
            def _():
                from_x(q - (k - 1))

            @pl.when((k > 1) & (q + k - 1 <= last))
            def _():
                from_x(q + k - 1)

        def finish_nodes():
            @pl.loop(0, chips)
            def _(s):
                for h in range(parts):
                    wait(node_block(s, h, 1 - c))

        def finish_halo():
            @pl.loop(0, chips)
            def _(s):
                for f in range(FACES):
                    wait(halo_block(s, f, 1 - c))

        def finish_sends():
            for s in range(chips):
                low = REACH[s] if s < last else chips
                high = REACH[last - s] if s else chips
                for h in range(parts):
                    block = node_block(s, h)
                    pl.when((q < last) & (s <= q))(lambda: copy(UP, block, ups).wait_send())
                    pl.when((q > 0) & (s >= q))(lambda: copy(DOWN, block, downs).wait_send())
                    copy(SIDE, block, sib).wait_send()
                for f in range(FACES):
                    block = halo_block(s, f)
                    across = copy(ACROSS, block, sib, face_ref.at[l, s, f])
                    copy(SIDE, block, sib).wait_send()
                    if f >= 2:
                        across.wait_send()
                    else:
                        pl.when(at_end(s))(across.wait_send)
                        beyond = copy(BEYOND, block, sib, face_ref.at[l, s, f])
                        pl.when(twice(s))(beyond.wait_send)
                        pl.when((q > low) & (q % 2 == 1))(lambda: copy(DOWN, block, downs).wait_send())
                        pl.when((last - q > high) & (q % 2 == 0))(lambda: copy(UP, block, ups).wait_send())

        return finish_nodes, finish_halo, finish_sends

    def project(l, out_ref, part, first, stop, bias):
        @pl.loop(first // STEP, stop // STEP)
        def _(i):
            base = pl.multiple_of(i * STEP, STEP)
            val = dot(
                table_ref[l, pl.ds(base, STEP), :],
                ew1_ref[l, part * width : (part + 1) * width, :],
            )
            if bias is not None:
                val = val + bias
            out_ref[pl.ds(2 * base, STEP, stride=2), :] = val[:, :half]
            out_ref[pl.ds(2 * base + 1, STEP, stride=2), :] = val[:, half:]

    def edge_phase(l):
        @pl.loop(0, edges // GROUP)
        def _(g):
            for u in range(GROUP):
                k = g * GROUP + u
                a = send_ref[k]
                b = recv_ref[k]
                at = pl.multiple_of(g * (2 * GROUP), 2 * GROUP) + 2 * u
                pre_ref[pl.ds(at, 2), :] = s_ref[pl.ds(2 * a, 2), :] + r_ref[pl.ds(2 * b, 2), :]

        pl.when(l == 0)(lambda: edge_load().wait())
        live = live_ref[0, 0]

        @pl.loop(0, edges // CHUNK)
        def _(i):
            base = pl.multiple_of(i * CHUNK, CHUNK)
            old = mid_ref[pl.ds(base, CHUNK), :]
            pre = dot(old, ew1_ref[l, :width, :])
            low = pre[:, :half] + pre_ref[pl.ds(2 * base, CHUNK, stride=2), :]
            high = pre[:, half:] + pre_ref[pl.ds(2 * base + 1, CHUNK, stride=2), :]
            hidden = jnp.maximum(jnp.concatenate([low, high], axis=1), 0.0).astype(BF16)
            message = layer_norm(dot(hidden, ew2_ref[l]), eg_ref[pl.ds(l, 1), :])
            slot = lax.broadcasted_iota(jnp.int32, (CHUNK, 1), 0) + base
            message = jnp.where(slot < live, message, 0.0)
            mid_ref[pl.ds(base, CHUNK), :] = (old.astype(F32) + message).astype(BF16)
            msg_ref[pl.ds(base, CHUNK), :] = message.astype(BF16)

        pl.when(l == LAYERS - 1)(lambda: edge_store().start())

    def scatter(owner):
        depth = 512
        ids = lax.broadcasted_iota(jnp.int32, (size, depth), 0) + owner * size
        acc = jnp.zeros((size, width), F32)
        for j in range(0, edges, depth):
            hit = ids == recv_row_ref[:, j : j + depth]
            acc = acc + dot(jnp.where(hit, 1.0, 0.0).astype(BF16), msg_ref[j : j + depth, :])
        return acc

    def reduce_phase(l, finish_sends):
        def pair_copy(t):
            return pltpu.make_async_remote_copy(
                src_ref=part_ref.at[l, t],
                dst_ref=pair_ref.at[l, t],
                send_sem=pair_sem.at[l, 0, t],
                recv_sem=pair_sem.at[l, 1, t],
                device_id=sib,
                device_id_type=MESH,
            )

        def sum_copy(t):
            return pltpu.make_async_remote_copy(
                src_ref=sums_ref.at[l, t],
                dst_ref=got_ref.at[l, t],
                send_sem=sum_sem.at[l, 0, t],
                recv_sem=sum_sem.at[l, 1, t],
                device_id=(d, peer(t)),
                device_id_type=MESH,
            )

        def turn(i):
            return (1 - i // 2) * (2 - i) + (i // 2) * (9 - 3 * i)

        def give(t):
            part_ref[l, t] = scatter(2 * ((q + t) % chips) + 1 - c).astype(BF16)
            pair_copy(t).start()

        def gain(t):
            total = scatter(peer(t))
            pair_copy(t).wait_recv()
            total = total + pair_ref[l, t].astype(F32)
            sum_ref[...] = total
            sums_ref[l, t] = total.astype(BF16)
            pl.when(t > 0)(lambda: sum_copy(t).start())

        give(2)

        @pl.loop(1, chips)
        def _(i):
            give(turn(i))
            gain(turn(i - 1))

        gain(0)
        finish_sends()
        own = node_ref[...]
        mine = sum_ref[...]
        pre = dot(own, nw1_ref[l, :width, :]) + nb1_ref[pl.ds(l, 1), :]
        for t in range(1, chips):
            sum_copy(t).wait_recv()
            mine = mine + got_ref[l, t].astype(F32)
        pre = pre + dot(mine.astype(BF16), nw1_ref[l, width:, :])
        hidden = jnp.maximum(pre, 0.0).astype(BF16)
        update = layer_norm(dot(hidden, nw2_ref[l]), ng_ref[pl.ds(l, 1), :])
        node_ref[...] = (own.astype(F32) + update).astype(BF16)
        for t in range(chips):
            pair_copy(t).wait_send()
            if t:
                sum_copy(t).wait_send()

    @pl.loop(0, LAYERS)
    def _(l):
        finish_nodes, finish_halo, finish_sends = exchange(l)
        finish_nodes()

        @pl.when(l == 0)
        def _():
            for load in loads():
                load.wait()

        project(l, s_ref, 1, 0, nodes, None)
        project(l, r_ref, 2, 0, nodes, eb1_ref[pl.ds(l, 1), :])
        finish_halo()
        project(l, s_ref, 1, nodes, table_ref.shape[1], None)
        edge_phase(l)
        reduce_phase(l, finish_sends)

    node_out_ref[...] = node_ref[...]
    edge_store().wait()
    for t in range(1, chips):
        list_copy(t).wait_send()


def settle_kernel(node_ref, edge_ref, node_out_ref, edge_out_ref, node_buf, edge_buf, sems):
    pieces = 4
    size = edge_ref.shape[0] // pieces
    moves = [(node_ref, node_buf, node_out_ref)]
    for i in range(pieces):
        part = pl.ds(i * size, size)
        moves.append((edge_ref.at[part], edge_buf.at[part], edge_out_ref.at[part]))
    loads = [
        pltpu.make_async_copy(move[0], move[1], sems.at[0, i]) for i, move in enumerate(moves)
    ]
    stores = [
        pltpu.make_async_copy(move[1], move[2], sems.at[1, i]) for i, move in enumerate(moves)
    ]
    for load in loads:
        load.start()
    for load, store in zip(loads, stores):
        load.wait()
        store.start()
    for store in stores:
        store.wait()


def shards(
    node_lat,
    edge_lat,
    senders,
    receivers,
    live_edges,
    send_rows,
    edge_w1,
    edge_b1,
    edge_w2,
    edge_gain,
    node_w1,
    node_b1,
    node_w2,
    node_gain,
):
    vmem = pl.BlockSpec(memory_space=pltpu.VMEM)
    smem = pl.BlockSpec(memory_space=pltpu.SMEM)
    hbm = pl.BlockSpec(memory_space=pl.ANY)
    dma = pltpu.SemaphoreType.DMA
    size, width = node_lat.shape
    edges = edge_lat.shape[0]
    count = lax.axis_size("edge")
    chips = count // 2
    nodes = count * size
    table = count * (size + FACES * HALO)
    blocks = table // HALO
    half = width // 2
    weights = (edge_w1, edge_b1, edge_w2, edge_gain, node_w1, node_b1, node_w2, node_gain)
    sums = pltpu.VMEM((LAYERS, chips, size, width), BF16)
    outs = (
        jax.ShapeDtypeStruct(node_lat.shape, BF16),
        jax.ShapeDtypeStruct(edge_lat.shape, BF16),
    )
    own, moved = pl.pallas_call(
        kernel,
        out_shape=outs,
        in_specs=[vmem, hbm, smem, smem, smem, vmem] + [hbm] * 9,
        out_specs=(vmem, hbm),
        scratch_shapes=[
            pltpu.VMEM((1, edges), jnp.int32),
            *(pltpu.VMEM(value.shape, value.dtype) for value in weights),
            pltpu.VMEM((LAYERS, table, width), BF16),
            pltpu.VMEM((LAYERS, chips, FACES, HALO, width), BF16),
            pltpu.VMEM((chips, FACES, HALO), jnp.int32),
            pltpu.VMEM((edges, width), BF16),
            pltpu.VMEM((2 * table, half), F32),
            pltpu.VMEM((2 * nodes, half), F32),
            pltpu.VMEM((2 * edges, half), F32),
            pltpu.VMEM((edges, width), BF16),
            sums,
            sums,
            sums,
            sums,
            pltpu.VMEM((size, width), F32),
            pltpu.VMEM((size, width), BF16),
            dma((LAYERS, 5, blocks)),
            dma((LAYERS, blocks)),
            dma((2, chips)),
            dma((LAYERS, 2, chips)),
            dma((LAYERS, 2, chips)),
            dma((2,)),
            dma((1 + len(weights),)),
        ],
        compiler_params=pltpu.CompilerParams(
            collective_id=0, has_side_effects=True, vmem_limit_bytes=56 * 2**20
        ),
        cost_estimate=pl.CostEstimate(
            flops=2 * 10**10, bytes_accessed=8 * 2**20, transcendentals=0
        ),
        name="graph_layers",
    )(
        node_lat,
        edge_lat,
        senders,
        receivers,
        live_edges,
        send_rows,
        receivers.reshape(1, -1),
        edge_w1,
        edge_b1,
        edge_w2,
        edge_gain,
        node_w1,
        node_b1,
        node_w2,
        node_gain,
    )
    return pl.pallas_call(
        settle_kernel,
        out_shape=outs,
        in_specs=[hbm, hbm],
        out_specs=(hbm, hbm),
        scratch_shapes=[
            pltpu.VMEM(node_lat.shape, BF16),
            pltpu.VMEM(edge_lat.shape, BF16),
            dma((2, 5)),
        ],
        name="settle",
    )(own, moved)


def solution(mesh):
    split = P(("dom", "edge"), None)
    in_specs = (
        split,
        split,
        P(("dom", "edge")),
        P(("dom", "edge")),
        P("dom", "edge"),
        P(("dom", "edge"), None, None),
    ) + (P(),) * 8
    return jax.shard_map(
        shards, mesh=mesh, in_specs=in_specs, out_specs=(split, split), check_vma=False
    )
```

```python
import jax
import jax.numpy as jnp
from jax import lax
from jax.experimental import pallas as pl
from jax.experimental.pallas import tpu as pltpu
from jax.sharding import PartitionSpec as P

LAYERS = 2
EPS = 1e-05
FACES = 4
HALO = 128
GROUP = 128
CHUNK = 1536
STEP = 1024
MESH = pl.DeviceIdType.MESH
BF16 = jnp.bfloat16
F32 = jnp.float32
UP, DOWN, SIDE, ACROSS = range(4)
REACH = (0, 1, 3)


def dot(a, b):
    return jnp.dot(a, b, preferred_element_type=F32)


def layer_norm(values, gain):
    center = values - jnp.mean(values, axis=-1, keepdims=True)
    spread = jnp.mean(center * center, axis=-1, keepdims=True)
    return center * lax.rsqrt(spread + EPS) * gain


def rows(start, size):
    return pl.ds(pl.multiple_of(start, size), size)


def kernel(
    own_ref,
    edge_ref,
    send_ref,
    recv_ref,
    live_ref,
    list_ref,
    recv_row_hbm,
    ew1_hbm,
    eb1_hbm,
    ew2_hbm,
    eg_hbm,
    nw1_hbm,
    nb1_hbm,
    nw2_hbm,
    ng_hbm,
    node_out_ref,
    edge_out_ref,
    recv_row_ref,
    ew1_ref,
    eb1_ref,
    ew2_ref,
    eg_ref,
    nw1_ref,
    nb1_ref,
    nw2_ref,
    ng_ref,
    table_ref,
    face_ref,
    lists_ref,
    mid_ref,
    s_ref,
    r_ref,
    pre_ref,
    msg_ref,
    part_ref,
    pair_ref,
    sums_ref,
    got_ref,
    sum_ref,
    node_ref,
    block_send,
    block_recv,
    list_sem,
    pair_sem,
    sum_sem,
    local_sem,
    load_sem,
):
    d = lax.axis_index("dom")
    e = lax.axis_index("edge")
    doms = lax.axis_size("dom")
    count = lax.axis_size("edge")
    chips = count // 2
    last = chips - 1
    stride = doms // 4
    size, width = own_ref.shape
    half = width // 2
    edges = edge_ref.shape[0]
    nodes = count * size
    parts = size // HALO
    q = e // 2
    c = e % 2
    sib = (d, 2 * q + 1 - c)
    ups = (d, e + 2)
    downs = (d, e - 2)
    there = [(d + s) % doms for s in (1, doms - 1, stride, doms - stride)]

    def peer(t):
        return 2 * ((q + t) % chips) + c

    def loads():
        pairs = (
            (ew1_hbm, ew1_ref),
            (eb1_hbm, eb1_ref),
            (ew2_hbm, ew2_ref),
            (eg_hbm, eg_ref),
            (recv_row_hbm, recv_row_ref),
            (nw1_hbm, nw1_ref),
            (nb1_hbm, nb1_ref),
            (nw2_hbm, nw2_ref),
            (ng_hbm, ng_ref),
        )
        return [
            pltpu.make_async_copy(src, dst, load_sem.at[i]) for i, (src, dst) in enumerate(pairs)
        ]

    def edge_load():
        return pltpu.make_async_copy(edge_ref, mid_ref, local_sem.at[0])

    for load in loads():
        load.start()
    edge_load().start()

    barrier = pltpu.get_barrier_semaphore()

    def greet(who):
        pl.semaphore_signal(barrier, inc=1, device_id=who, device_id_type=MESH)

    greet(sib)
    for t in range(1, chips):
        greet((d, peer(t)))
    for f in (2, 3):
        greet((there[f], e))
    for f in (0, 1):
        greet((there[f], 2 * (last - q) + c))
    pl.semaphore_wait(barrier, 1 + (chips - 1) + 2 + 2)

    def edge_store():
        return pltpu.make_async_copy(mid_ref, edge_out_ref, local_sem.at[1])

    def list_copy(t):
        return pltpu.make_async_remote_copy(
            src_ref=list_ref,
            dst_ref=lists_ref.at[pl.ds(q, 1)],
            send_sem=list_sem.at[0, t],
            recv_sem=list_sem.at[1, t],
            device_id=(d, peer(t)),
            device_id_type=MESH,
        )

    lists_ref[pl.ds(q, 1)] = list_ref[...]
    for t in range(1, chips):
        list_copy(t).start()
    node_ref[...] = own_ref[...]

    def exchange(l):
        def node_block(s, h, core=c):
            return (2 * s + core) * parts + h

        def halo_block(s, f, core=c):
            return count * parts + (2 * s + core) * FACES + f

        def block_at(block):
            return table_ref.at[l, rows(block * HALO, HALO), :]

        def copy(kind, block, who, src=None):
            return pltpu.make_async_remote_copy(
                src_ref=block_at(block) if src is None else src,
                dst_ref=block_at(block),
                send_sem=block_send.at[l, kind, block],
                recv_sem=block_recv.at[l, block],
                device_id=who,
                device_id_type=MESH,
            )

        def start(cond, kind, block, who):
            if cond is None:
                copy(kind, block, who).start()
            else:
                pl.when(cond)(lambda: copy(kind, block, who).start())

        def wait(block):
            copy(SIDE, block, sib).wait_recv()

        ids = lax.broadcasted_iota(jnp.int32, (size, HALO), 0)

        def pick(s, f, who):
            hit = jnp.where(ids == lists_ref[s, pl.ds(f, 1), :], 1.0, 0.0).astype(BF16)
            values = table_ref[l, rows((2 * s + c) * size, size), :]
            face_ref[l, s, f] = lax.dot_general(
                hit, values, (((0,), (0,)), ((), ())), preferred_element_type=F32
            ).astype(BF16)
            copy(ACROSS, halo_block(s, f), who, face_ref.at[l, s, f]).start()

        def at_end(s):
            return ((q == 0) & (s != last)) | ((q == last) & (s != 0))

        def available(s):
            @pl.when(at_end(s))
            def _():
                @pl.loop(0, 2)
                def _(f):
                    pick(s, f, ((d + doms + 1 - 2 * f) % doms, 2 * (last - q) + c))

            @pl.loop(2, FACES)
            def _(f):
                pick(s, f, ((d + doms + stride * (5 - 2 * f)) % doms, e))

        table_ref[l, rows(e * size, size), :] = node_ref[...]
        for h in range(parts):
            start(q < last, UP, node_block(q, h), ups)
            start(q > 0, DOWN, node_block(q, h), downs)
        for h in range(parts):
            start(None, SIDE, node_block(q, h), sib)
        available(q)

        def from_line(s, onward, kind, who):
            for h in range(parts):
                block = node_block(s, h)
                wait(block)
                start(onward, kind, block, who)
                start(None, SIDE, block, sib)

            @pl.when(l == 0)
            def _():
                list_copy((q + chips - s) % chips).wait_recv()

            available(s)

        def from_x(s):
            for f in (2, 3):
                block = halo_block(s, f)
                wait(block)
                start(None, SIDE, block, sib)

        def from_z(s, onward, kind, who):
            for f in (0, 1):
                block = halo_block(s, f)
                wait(block)
                start(onward, kind, block, who)
                start(None, SIDE, block, sib)

        @pl.loop(1, chips + 1)
        def _(k):
            for kind, who in ((DOWN, downs), (UP, ups)):
                for a, least in enumerate(REACH):
                    place = chips + a - k
                    mine = q if kind == DOWN else last - q
                    s = a if kind == DOWN else last - a

                    @pl.when((mine == place) & (place >= least))
                    def _():
                        from_z(s, place > least, kind, who)

            @pl.when((k < chips) & (q >= k))
            def _():
                from_line(q - k, q < last, UP, ups)

            @pl.when((k < chips) & (q + k <= last))
            def _():
                from_line(q + k, q > 0, DOWN, downs)

            @pl.when(q >= k - 1)
            def _():
                from_x(q - (k - 1))

            @pl.when((k > 1) & (q + k - 1 <= last))
            def _():
                from_x(q + k - 1)

        def finish_nodes():
            @pl.loop(0, chips)
            def _(s):
                for h in range(parts):
                    wait(node_block(s, h, 1 - c))

        def finish_halo():
            @pl.loop(0, chips)
            def _(s):
                for f in range(FACES):
                    wait(halo_block(s, f, 1 - c))

        def finish_sends():
            for s in range(chips):
                low = REACH[s] if s < last else chips
                high = REACH[last - s] if s else chips
                for h in range(parts):
                    block = node_block(s, h)
                    pl.when((q < last) & (s <= q))(lambda: copy(UP, block, ups).wait_send())
                    pl.when((q > 0) & (s >= q))(lambda: copy(DOWN, block, downs).wait_send())
                    copy(SIDE, block, sib).wait_send()
                for f in range(FACES):
                    block = halo_block(s, f)
                    across = copy(ACROSS, block, sib, face_ref.at[l, s, f])
                    copy(SIDE, block, sib).wait_send()
                    if f >= 2:
                        across.wait_send()
                    else:
                        pl.when(at_end(s))(across.wait_send)
                        pl.when(q > low)(lambda: copy(DOWN, block, downs).wait_send())
                        pl.when(last - q > high)(lambda: copy(UP, block, ups).wait_send())

        return finish_nodes, finish_halo, finish_sends

    def project(l, out_ref, part, first, stop, bias):
        @pl.loop(first // STEP, stop // STEP)
        def _(i):
            base = pl.multiple_of(i * STEP, STEP)
            val = dot(
                table_ref[l, pl.ds(base, STEP), :],
                ew1_ref[l, part * width : (part + 1) * width, :],
            )
            if bias is not None:
                val = val + bias
            out_ref[pl.ds(2 * base, STEP, stride=2), :] = val[:, :half]
            out_ref[pl.ds(2 * base + 1, STEP, stride=2), :] = val[:, half:]

    def edge_phase(l):
        @pl.loop(0, edges // GROUP)
        def _(g):
            for u in range(GROUP):
                k = g * GROUP + u
                a = send_ref[k]
                b = recv_ref[k]
                at = pl.multiple_of(g * (2 * GROUP), 2 * GROUP) + 2 * u
                pre_ref[pl.ds(at, 2), :] = s_ref[pl.ds(2 * a, 2), :] + r_ref[pl.ds(2 * b, 2), :]

        pl.when(l == 0)(lambda: edge_load().wait())
        live = live_ref[0, 0]

        @pl.loop(0, edges // CHUNK)
        def _(i):
            base = pl.multiple_of(i * CHUNK, CHUNK)
            old = mid_ref[pl.ds(base, CHUNK), :]
            pre = dot(old, ew1_ref[l, :width, :])
            low = pre[:, :half] + pre_ref[pl.ds(2 * base, CHUNK, stride=2), :]
            high = pre[:, half:] + pre_ref[pl.ds(2 * base + 1, CHUNK, stride=2), :]
            hidden = jnp.maximum(jnp.concatenate([low, high], axis=1), 0.0).astype(BF16)
            message = layer_norm(dot(hidden, ew2_ref[l]), eg_ref[pl.ds(l, 1), :])
            slot = lax.broadcasted_iota(jnp.int32, (CHUNK, 1), 0) + base
            message = jnp.where(slot < live, message, 0.0)
            mid_ref[pl.ds(base, CHUNK), :] = (old.astype(F32) + message).astype(BF16)
            msg_ref[pl.ds(base, CHUNK), :] = message.astype(BF16)

        pl.when(l == LAYERS - 1)(lambda: edge_store().start())

    def scatter(owner):
        depth = 512
        ids = lax.broadcasted_iota(jnp.int32, (size, depth), 0) + owner * size
        acc = jnp.zeros((size, width), F32)
        for j in range(0, edges, depth):
            hit = ids == recv_row_ref[:, j : j + depth]
            acc = acc + dot(jnp.where(hit, 1.0, 0.0).astype(BF16), msg_ref[j : j + depth, :])
        return acc

    def reduce_phase(l, finish_sends):
        def pair_copy(t):
            return pltpu.make_async_remote_copy(
                src_ref=part_ref.at[l, t],
                dst_ref=pair_ref.at[l, t],
                send_sem=pair_sem.at[l, 0, t],
                recv_sem=pair_sem.at[l, 1, t],
                device_id=sib,
                device_id_type=MESH,
            )

        def sum_copy(t):
            return pltpu.make_async_remote_copy(
                src_ref=sums_ref.at[l, t],
                dst_ref=got_ref.at[l, t],
                send_sem=sum_sem.at[l, 0, t],
                recv_sem=sum_sem.at[l, 1, t],
                device_id=(d, peer(t)),
                device_id_type=MESH,
            )

        def turn(i):
            return (1 - i // 2) * (2 - i) + (i // 2) * (9 - 3 * i)

        def give(t):
            part_ref[l, t] = scatter(2 * ((q + t) % chips) + 1 - c).astype(BF16)
            pair_copy(t).start()

        def gain(t):
            total = scatter(peer(t))
            pair_copy(t).wait_recv()
            total = total + pair_ref[l, t].astype(F32)
            sum_ref[...] = total
            sums_ref[l, t] = total.astype(BF16)
            pl.when(t > 0)(lambda: sum_copy(t).start())

        give(2)

        @pl.loop(1, chips)
        def _(i):
            give(turn(i))
            gain(turn(i - 1))

        gain(0)
        finish_sends()
        own = node_ref[...]
        mine = sum_ref[...]
        pre = dot(own, nw1_ref[l, :width, :]) + nb1_ref[pl.ds(l, 1), :]
        for t in range(1, chips):
            sum_copy(t).wait_recv()
            mine = mine + got_ref[l, t].astype(F32)
        pre = pre + dot(mine.astype(BF16), nw1_ref[l, width:, :])
        hidden = jnp.maximum(pre, 0.0).astype(BF16)
        update = layer_norm(dot(hidden, nw2_ref[l]), ng_ref[pl.ds(l, 1), :])
        node_ref[...] = (own.astype(F32) + update).astype(BF16)
        for t in range(chips):
            pair_copy(t).wait_send()
            if t:
                sum_copy(t).wait_send()

    @pl.loop(0, LAYERS)
    def _(l):
        finish_nodes, finish_halo, finish_sends = exchange(l)
        finish_nodes()

        @pl.when(l == 0)
        def _():
            for load in loads():
                load.wait()

        project(l, s_ref, 1, 0, nodes, None)
        project(l, r_ref, 2, 0, nodes, eb1_ref[pl.ds(l, 1), :])
        finish_halo()
        project(l, s_ref, 1, nodes, table_ref.shape[1], None)
        edge_phase(l)
        reduce_phase(l, finish_sends)

    node_out_ref[...] = node_ref[...]
    edge_store().wait()
    for t in range(1, chips):
        list_copy(t).wait_send()


def settle_kernel(node_ref, edge_ref, node_out_ref, edge_out_ref, node_buf, edge_buf, sems):
    pieces = 4
    size = edge_ref.shape[0] // pieces
    moves = [(node_ref, node_buf, node_out_ref)]
    for i in range(pieces):
        part = pl.ds(i * size, size)
        moves.append((edge_ref.at[part], edge_buf.at[part], edge_out_ref.at[part]))
    loads = [
        pltpu.make_async_copy(move[0], move[1], sems.at[0, i]) for i, move in enumerate(moves)
    ]
    stores = [
        pltpu.make_async_copy(move[1], move[2], sems.at[1, i]) for i, move in enumerate(moves)
    ]
    for load in loads:
        load.start()
    for load, store in zip(loads, stores):
        load.wait()
        store.start()
    for store in stores:
        store.wait()


def shards(
    node_lat,
    edge_lat,
    senders,
    receivers,
    live_edges,
    send_rows,
    edge_w1,
    edge_b1,
    edge_w2,
    edge_gain,
    node_w1,
    node_b1,
    node_w2,
    node_gain,
):
    vmem = pl.BlockSpec(memory_space=pltpu.VMEM)
    smem = pl.BlockSpec(memory_space=pltpu.SMEM)
    hbm = pl.BlockSpec(memory_space=pl.ANY)
    dma = pltpu.SemaphoreType.DMA
    size, width = node_lat.shape
    edges = edge_lat.shape[0]
    count = lax.axis_size("edge")
    chips = count // 2
    nodes = count * size
    table = count * (size + FACES * HALO)
    blocks = table // HALO
    half = width // 2
    weights = (edge_w1, edge_b1, edge_w2, edge_gain, node_w1, node_b1, node_w2, node_gain)
    sums = pltpu.VMEM((LAYERS, chips, size, width), BF16)
    outs = (
        jax.ShapeDtypeStruct(node_lat.shape, BF16),
        jax.ShapeDtypeStruct(edge_lat.shape, BF16),
    )
    own, moved = pl.pallas_call(
        kernel,
        out_shape=outs,
        in_specs=[vmem, hbm, smem, smem, smem, vmem] + [hbm] * 9,
        out_specs=(vmem, hbm),
        scratch_shapes=[
            pltpu.VMEM((1, edges), jnp.int32),
            *(pltpu.VMEM(value.shape, value.dtype) for value in weights),
            pltpu.VMEM((LAYERS, table, width), BF16),
            pltpu.VMEM((LAYERS, chips, FACES, HALO, width), BF16),
            pltpu.VMEM((chips, FACES, HALO), jnp.int32),
            pltpu.VMEM((edges, width), BF16),
            pltpu.VMEM((2 * table, half), F32),
            pltpu.VMEM((2 * nodes, half), F32),
            pltpu.VMEM((2 * edges, half), F32),
            pltpu.VMEM((edges, width), BF16),
            sums,
            sums,
            sums,
            sums,
            pltpu.VMEM((size, width), F32),
            pltpu.VMEM((size, width), BF16),
            dma((LAYERS, 4, blocks)),
            dma((LAYERS, blocks)),
            dma((2, chips)),
            dma((LAYERS, 2, chips)),
            dma((LAYERS, 2, chips)),
            dma((2,)),
            dma((1 + len(weights),)),
        ],
        compiler_params=pltpu.CompilerParams(
            collective_id=0, has_side_effects=True, vmem_limit_bytes=56 * 2**20
        ),
        cost_estimate=pl.CostEstimate(
            flops=2 * 10**10, bytes_accessed=8 * 2**20, transcendentals=0
        ),
        name="graph_layers",
    )(
        node_lat,
        edge_lat,
        senders,
        receivers,
        live_edges,
        send_rows,
        receivers.reshape(1, -1),
        edge_w1,
        edge_b1,
        edge_w2,
        edge_gain,
        node_w1,
        node_b1,
        node_w2,
        node_gain,
    )
    return pl.pallas_call(
        settle_kernel,
        out_shape=outs,
        in_specs=[hbm, hbm],
        out_specs=(hbm, hbm),
        scratch_shapes=[
            pltpu.VMEM(node_lat.shape, BF16),
            pltpu.VMEM(edge_lat.shape, BF16),
            dma((2, 5)),
        ],
        name="settle",
    )(own, moved)


def solution(mesh):
    split = P(("dom", "edge"), None)
    in_specs = (
        split,
        split,
        P(("dom", "edge")),
        P(("dom", "edge")),
        P("dom", "edge"),
        P(("dom", "edge"), None, None),
    ) + (P(),) * 8
    return jax.shard_map(
        shards, mesh=mesh, in_specs=in_specs, out_specs=(split, split), check_vma=False
    )
```

```python
import jax
import jax.numpy as jnp
from jax import lax
from jax.experimental import pallas as pl
from jax.experimental.pallas import tpu as pltpu
from jax.sharding import PartitionSpec as P

LAYERS = 2
EPS = 1e-05
FACES = 4
HALO = 128
GROUP = 128
CHUNK = 1536
STEP = 1024
MESH = pl.DeviceIdType.MESH
BF16 = jnp.bfloat16
F32 = jnp.float32
UP, DOWN, SIDE, ACROSS = range(4)
REACH = (0, 1, 3)


def dot(a, b):
    return jnp.dot(a, b, preferred_element_type=F32)


def layer_norm(values, gain):
    center = values - jnp.mean(values, axis=-1, keepdims=True)
    spread = jnp.mean(center * center, axis=-1, keepdims=True)
    return center * lax.rsqrt(spread + EPS) * gain


def rows(start, size):
    return pl.ds(pl.multiple_of(start, size), size)


def kernel(
    own_ref,
    edge_ref,
    send_ref,
    recv_ref,
    live_ref,
    list_ref,
    recv_row_hbm,
    ew1_hbm,
    eb1_hbm,
    ew2_hbm,
    eg_hbm,
    nw1_hbm,
    nb1_hbm,
    nw2_hbm,
    ng_hbm,
    node_out_ref,
    edge_out_ref,
    recv_row_ref,
    ew1_ref,
    eb1_ref,
    ew2_ref,
    eg_ref,
    nw1_ref,
    nb1_ref,
    nw2_ref,
    ng_ref,
    table_ref,
    face_ref,
    lists_ref,
    mid_ref,
    s_ref,
    r_ref,
    pre_ref,
    msg_ref,
    part_ref,
    pair_ref,
    sums_ref,
    got_ref,
    sum_ref,
    node_ref,
    block_send,
    block_recv,
    list_sem,
    pair_sem,
    sum_sem,
    local_sem,
    load_sem,
):
    d = lax.axis_index("dom")
    e = lax.axis_index("edge")
    doms = lax.axis_size("dom")
    count = lax.axis_size("edge")
    chips = count // 2
    last = chips - 1
    stride = doms // 4
    size, width = own_ref.shape
    half = width // 2
    edges = edge_ref.shape[0]
    nodes = count * size
    parts = size // HALO
    q = e // 2
    c = e % 2
    sib = (d, 2 * q + 1 - c)
    ups = (d, e + 2)
    downs = (d, e - 2)
    there = [(d + s) % doms for s in (1, doms - 1, stride, doms - stride)]

    def peer(t):
        return 2 * ((q + t) % chips) + c

    def loads():
        pairs = (
            (ew1_hbm, ew1_ref),
            (eb1_hbm, eb1_ref),
            (ew2_hbm, ew2_ref),
            (eg_hbm, eg_ref),
            (recv_row_hbm, recv_row_ref),
            (nw1_hbm, nw1_ref),
            (nb1_hbm, nb1_ref),
            (nw2_hbm, nw2_ref),
            (ng_hbm, ng_ref),
        )
        return [
            pltpu.make_async_copy(src, dst, load_sem.at[i]) for i, (src, dst) in enumerate(pairs)
        ]

    def edge_load():
        return pltpu.make_async_copy(edge_ref, mid_ref, local_sem.at[0])

    for load in loads():
        load.start()
    edge_load().start()

    barrier = pltpu.get_barrier_semaphore()

    def greet(who):
        pl.semaphore_signal(barrier, inc=1, device_id=who, device_id_type=MESH)

    greet(sib)
    for t in range(1, chips):
        greet((d, peer(t)))
    for f in (2, 3):
        greet((there[f], e))
    for f in (0, 1):
        greet((there[f], 2 * (last - q) + c))
    pl.semaphore_wait(barrier, 1 + (chips - 1) + 2 + 2)

    def edge_store():
        return pltpu.make_async_copy(mid_ref, edge_out_ref, local_sem.at[1])

    def list_copy(t):
        return pltpu.make_async_remote_copy(
            src_ref=list_ref,
            dst_ref=lists_ref.at[pl.ds(q, 1)],
            send_sem=list_sem.at[0, t],
            recv_sem=list_sem.at[1, t],
            device_id=(d, peer(t)),
            device_id_type=MESH,
        )

    lists_ref[pl.ds(q, 1)] = list_ref[...]
    for t in range(1, chips):
        list_copy(t).start()
    node_ref[...] = own_ref[...]

    def exchange(l):
        def node_block(s, h, core=c):
            return (2 * s + core) * parts + h

        def halo_block(s, f, core=c):
            return count * parts + (2 * s + core) * FACES + f

        def block_at(block):
            return table_ref.at[l, rows(block * HALO, HALO), :]

        def copy(kind, block, who, src=None):
            return pltpu.make_async_remote_copy(
                src_ref=block_at(block) if src is None else src,
                dst_ref=block_at(block),
                send_sem=block_send.at[l, kind, block],
                recv_sem=block_recv.at[l, block],
                device_id=who,
                device_id_type=MESH,
            )

        def start(cond, kind, block, who):
            if cond is None:
                copy(kind, block, who).start()
            else:
                pl.when(cond)(lambda: copy(kind, block, who).start())

        def wait(block):
            copy(SIDE, block, sib).wait_recv()

        ids = lax.broadcasted_iota(jnp.int32, (size, HALO), 0)

        def pick(s, f, who):
            hit = jnp.where(ids == lists_ref[s, pl.ds(f, 1), :], 1.0, 0.0).astype(BF16)
            values = table_ref[l, rows((2 * s + c) * size, size), :]
            face_ref[l, s, f] = lax.dot_general(
                hit, values, (((0,), (0,)), ((), ())), preferred_element_type=F32
            ).astype(BF16)
            copy(ACROSS, halo_block(s, f), who, face_ref.at[l, s, f]).start()

        def at_end(s):
            return ((q == 0) & (s != last)) | ((q == last) & (s != 0))

        def available(s):
            @pl.when(at_end(s))
            def _():
                @pl.loop(0, 2)
                def _(f):
                    pick(s, f, ((d + doms + 1 - 2 * f) % doms, 2 * (last - q) + c))

            @pl.loop(2, FACES)
            def _(f):
                pick(s, f, ((d + doms + stride * (5 - 2 * f)) % doms, e))

        table_ref[l, rows(e * size, size), :] = node_ref[...]
        for h in range(parts):
            start(q < last, UP, node_block(q, h), ups)
            start(q > 0, DOWN, node_block(q, h), downs)
        for h in range(parts):
            start(None, SIDE, node_block(q, h), sib)
        available(q)

        def from_line(s, onward, kind, who):
            for h in range(parts):
                block = node_block(s, h)
                wait(block)
                start(onward, kind, block, who)
                start(None, SIDE, block, sib)

            @pl.when(l == 0)
            def _():
                list_copy((q + chips - s) % chips).wait_recv()

            available(s)

        def from_x(s):
            for f in (2, 3):
                block = halo_block(s, f)
                wait(block)
                start(None, SIDE, block, sib)

        def from_z(s, onward, kind, who):
            for f in (0, 1):
                block = halo_block(s, f)
                wait(block)
                start(onward, kind, block, who)
                start(None, SIDE, block, sib)

        @pl.loop(1, chips + 1)
        def _(k):
            @pl.when((k < chips) & (q >= k))
            def _():
                from_line(q - k, q < last, UP, ups)

            @pl.when((k < chips) & (q + k <= last))
            def _():
                from_line(q + k, q > 0, DOWN, downs)

            for kind, who in ((DOWN, downs), (UP, ups)):
                for a, least in enumerate(REACH):
                    place = chips + a - k
                    mine = q if kind == DOWN else last - q
                    s = a if kind == DOWN else last - a

                    @pl.when((mine == place) & (place >= least))
                    def _():
                        from_z(s, place > least, kind, who)

            @pl.when(q >= k - 1)
            def _():
                from_x(q - (k - 1))

            @pl.when((k > 1) & (q + k - 1 <= last))
            def _():
                from_x(q + k - 1)

        def finish_nodes():
            @pl.loop(0, chips)
            def _(s):
                for h in range(parts):
                    wait(node_block(s, h, 1 - c))

        def finish_halo():
            @pl.loop(0, chips)
            def _(s):
                for f in range(FACES):
                    wait(halo_block(s, f, 1 - c))

        def finish_sends():
            for s in range(chips):
                low = REACH[s] if s < last else chips
                high = REACH[last - s] if s else chips
                for h in range(parts):
                    block = node_block(s, h)
                    pl.when((q < last) & (s <= q))(lambda: copy(UP, block, ups).wait_send())
                    pl.when((q > 0) & (s >= q))(lambda: copy(DOWN, block, downs).wait_send())
                    copy(SIDE, block, sib).wait_send()
                for f in range(FACES):
                    block = halo_block(s, f)
                    across = copy(ACROSS, block, sib, face_ref.at[l, s, f])
                    copy(SIDE, block, sib).wait_send()
                    if f >= 2:
                        across.wait_send()
                    else:
                        pl.when(at_end(s))(across.wait_send)
                        pl.when(q > low)(lambda: copy(DOWN, block, downs).wait_send())
                        pl.when(last - q > high)(lambda: copy(UP, block, ups).wait_send())

        return finish_nodes, finish_halo, finish_sends

    def project(l, out_ref, part, first, stop, bias):
        @pl.loop(first // STEP, stop // STEP)
        def _(i):
            base = pl.multiple_of(i * STEP, STEP)
            val = dot(
                table_ref[l, pl.ds(base, STEP), :],
                ew1_ref[l, part * width : (part + 1) * width, :],
            )
            if bias is not None:
                val = val + bias
            out_ref[pl.ds(2 * base, STEP, stride=2), :] = val[:, :half]
            out_ref[pl.ds(2 * base + 1, STEP, stride=2), :] = val[:, half:]

    def edge_phase(l):
        @pl.loop(0, edges // GROUP)
        def _(g):
            for u in range(GROUP):
                k = g * GROUP + u
                a = send_ref[k]
                b = recv_ref[k]
                at = pl.multiple_of(g * (2 * GROUP), 2 * GROUP) + 2 * u
                pre_ref[pl.ds(at, 2), :] = s_ref[pl.ds(2 * a, 2), :] + r_ref[pl.ds(2 * b, 2), :]

        pl.when(l == 0)(lambda: edge_load().wait())
        live = live_ref[0, 0]

        @pl.loop(0, edges // CHUNK)
        def _(i):
            base = pl.multiple_of(i * CHUNK, CHUNK)
            old = mid_ref[pl.ds(base, CHUNK), :]
            pre = dot(old, ew1_ref[l, :width, :])
            low = pre[:, :half] + pre_ref[pl.ds(2 * base, CHUNK, stride=2), :]
            high = pre[:, half:] + pre_ref[pl.ds(2 * base + 1, CHUNK, stride=2), :]
            hidden = jnp.maximum(jnp.concatenate([low, high], axis=1), 0.0).astype(BF16)
            message = layer_norm(dot(hidden, ew2_ref[l]), eg_ref[pl.ds(l, 1), :])
            slot = lax.broadcasted_iota(jnp.int32, (CHUNK, 1), 0) + base
            message = jnp.where(slot < live, message, 0.0)
            mid_ref[pl.ds(base, CHUNK), :] = (old.astype(F32) + message).astype(BF16)
            msg_ref[pl.ds(base, CHUNK), :] = message.astype(BF16)

        pl.when(l == LAYERS - 1)(lambda: edge_store().start())

    def scatter(owner):
        depth = 512
        ids = lax.broadcasted_iota(jnp.int32, (size, depth), 0) + owner * size
        acc = jnp.zeros((size, width), F32)
        for j in range(0, edges, depth):
            hit = ids == recv_row_ref[:, j : j + depth]
            acc = acc + dot(jnp.where(hit, 1.0, 0.0).astype(BF16), msg_ref[j : j + depth, :])
        return acc

    def reduce_phase(l, finish_sends):
        def pair_copy(t):
            return pltpu.make_async_remote_copy(
                src_ref=part_ref.at[l, t],
                dst_ref=pair_ref.at[l, t],
                send_sem=pair_sem.at[l, 0, t],
                recv_sem=pair_sem.at[l, 1, t],
                device_id=sib,
                device_id_type=MESH,
            )

        def sum_copy(t):
            return pltpu.make_async_remote_copy(
                src_ref=sums_ref.at[l, t],
                dst_ref=got_ref.at[l, t],
                send_sem=sum_sem.at[l, 0, t],
                recv_sem=sum_sem.at[l, 1, t],
                device_id=(d, peer(t)),
                device_id_type=MESH,
            )

        def turn(i):
            return (1 - i // 2) * (2 - i) + (i // 2) * (9 - 3 * i)

        def give(t):
            part_ref[l, t] = scatter(2 * ((q + t) % chips) + 1 - c).astype(BF16)
            pair_copy(t).start()

        def gain(t):
            total = scatter(peer(t))
            pair_copy(t).wait_recv()
            total = total + pair_ref[l, t].astype(F32)
            sum_ref[...] = total
            sums_ref[l, t] = total.astype(BF16)
            pl.when(t > 0)(lambda: sum_copy(t).start())

        give(2)

        @pl.loop(1, chips)
        def _(i):
            give(turn(i))
            gain(turn(i - 1))

        gain(0)
        finish_sends()
        own = node_ref[...]
        mine = sum_ref[...]
        pre = dot(own, nw1_ref[l, :width, :]) + nb1_ref[pl.ds(l, 1), :]
        for t in range(1, chips):
            sum_copy(t).wait_recv()
            mine = mine + got_ref[l, t].astype(F32)
        pre = pre + dot(mine.astype(BF16), nw1_ref[l, width:, :])
        hidden = jnp.maximum(pre, 0.0).astype(BF16)
        update = layer_norm(dot(hidden, nw2_ref[l]), ng_ref[pl.ds(l, 1), :])
        node_ref[...] = (own.astype(F32) + update).astype(BF16)
        for t in range(chips):
            pair_copy(t).wait_send()
            if t:
                sum_copy(t).wait_send()

    @pl.loop(0, LAYERS)
    def _(l):
        finish_nodes, finish_halo, finish_sends = exchange(l)
        finish_nodes()

        @pl.when(l == 0)
        def _():
            for load in loads():
                load.wait()

        project(l, s_ref, 1, 0, nodes, None)
        project(l, r_ref, 2, 0, nodes, eb1_ref[pl.ds(l, 1), :])
        finish_halo()
        project(l, s_ref, 1, nodes, table_ref.shape[1], None)
        edge_phase(l)
        reduce_phase(l, finish_sends)

    node_out_ref[...] = node_ref[...]
    edge_store().wait()
    for t in range(1, chips):
        list_copy(t).wait_send()


def settle_kernel(node_ref, edge_ref, node_out_ref, edge_out_ref, node_buf, edge_buf, sems):
    pieces = 4
    size = edge_ref.shape[0] // pieces
    moves = [(node_ref, node_buf, node_out_ref)]
    for i in range(pieces):
        part = pl.ds(i * size, size)
        moves.append((edge_ref.at[part], edge_buf.at[part], edge_out_ref.at[part]))
    loads = [
        pltpu.make_async_copy(move[0], move[1], sems.at[0, i]) for i, move in enumerate(moves)
    ]
    stores = [
        pltpu.make_async_copy(move[1], move[2], sems.at[1, i]) for i, move in enumerate(moves)
    ]
    for load in loads:
        load.start()
    for load, store in zip(loads, stores):
        load.wait()
        store.start()
    for store in stores:
        store.wait()


def shards(
    node_lat,
    edge_lat,
    senders,
    receivers,
    live_edges,
    send_rows,
    edge_w1,
    edge_b1,
    edge_w2,
    edge_gain,
    node_w1,
    node_b1,
    node_w2,
    node_gain,
):
    vmem = pl.BlockSpec(memory_space=pltpu.VMEM)
    smem = pl.BlockSpec(memory_space=pltpu.SMEM)
    hbm = pl.BlockSpec(memory_space=pl.ANY)
    dma = pltpu.SemaphoreType.DMA
    size, width = node_lat.shape
    edges = edge_lat.shape[0]
    count = lax.axis_size("edge")
    chips = count // 2
    nodes = count * size
    table = count * (size + FACES * HALO)
    blocks = table // HALO
    half = width // 2
    weights = (edge_w1, edge_b1, edge_w2, edge_gain, node_w1, node_b1, node_w2, node_gain)
    sums = pltpu.VMEM((LAYERS, chips, size, width), BF16)
    outs = (
        jax.ShapeDtypeStruct(node_lat.shape, BF16),
        jax.ShapeDtypeStruct(edge_lat.shape, BF16),
    )
    own, moved = pl.pallas_call(
        kernel,
        out_shape=outs,
        in_specs=[vmem, hbm, smem, smem, smem, vmem] + [hbm] * 9,
        out_specs=(vmem, hbm),
        scratch_shapes=[
            pltpu.VMEM((1, edges), jnp.int32),
            *(pltpu.VMEM(value.shape, value.dtype) for value in weights),
            pltpu.VMEM((LAYERS, table, width), BF16),
            pltpu.VMEM((LAYERS, chips, FACES, HALO, width), BF16),
            pltpu.VMEM((chips, FACES, HALO), jnp.int32),
            pltpu.VMEM((edges, width), BF16),
            pltpu.VMEM((2 * table, half), F32),
            pltpu.VMEM((2 * nodes, half), F32),
            pltpu.VMEM((2 * edges, half), F32),
            pltpu.VMEM((edges, width), BF16),
            sums,
            sums,
            sums,
            sums,
            pltpu.VMEM((size, width), F32),
            pltpu.VMEM((size, width), BF16),
            dma((LAYERS, 4, blocks)),
            dma((LAYERS, blocks)),
            dma((2, chips)),
            dma((LAYERS, 2, chips)),
            dma((LAYERS, 2, chips)),
            dma((2,)),
            dma((1 + len(weights),)),
        ],
        compiler_params=pltpu.CompilerParams(
            collective_id=0, has_side_effects=True, vmem_limit_bytes=56 * 2**20
        ),
        cost_estimate=pl.CostEstimate(
            flops=2 * 10**10, bytes_accessed=8 * 2**20, transcendentals=0
        ),
        name="graph_layers",
    )(
        node_lat,
        edge_lat,
        senders,
        receivers,
        live_edges,
        send_rows,
        receivers.reshape(1, -1),
        edge_w1,
        edge_b1,
        edge_w2,
        edge_gain,
        node_w1,
        node_b1,
        node_w2,
        node_gain,
    )
    return pl.pallas_call(
        settle_kernel,
        out_shape=outs,
        in_specs=[hbm, hbm],
        out_specs=(hbm, hbm),
        scratch_shapes=[
            pltpu.VMEM(node_lat.shape, BF16),
            pltpu.VMEM(edge_lat.shape, BF16),
            dma((2, 5)),
        ],
        name="settle",
    )(own, moved)


def solution(mesh):
    split = P(("dom", "edge"), None)
    in_specs = (
        split,
        split,
        P(("dom", "edge")),
        P(("dom", "edge")),
        P("dom", "edge"),
        P(("dom", "edge"), None, None),
    ) + (P(),) * 8
    return jax.shard_map(
        shards, mesh=mesh, in_specs=in_specs, out_specs=(split, split), check_vma=False
    )
```

```python
import jax
import jax.numpy as jnp
from jax import lax
from jax.experimental import pallas as pl
from jax.experimental.pallas import tpu as pltpu
from jax.sharding import PartitionSpec as P

LAYERS = 2
EPS = 1e-05
FACES = 4
HALO = 128
GROUP = 128
CHUNK = 1536
STEP = 1024
MESH = pl.DeviceIdType.MESH
BF16 = jnp.bfloat16
F32 = jnp.float32
UP, DOWN, SIDE, ACROSS = range(4)
REACH = (0, 1, 3)


def dot(a, b):
    return jnp.dot(a, b, preferred_element_type=F32)


def layer_norm(values, gain):
    center = values - jnp.mean(values, axis=-1, keepdims=True)
    spread = jnp.mean(center * center, axis=-1, keepdims=True)
    return center * lax.rsqrt(spread + EPS) * gain


def rows(start, size):
    return pl.ds(pl.multiple_of(start, size), size)


def kernel(
    own_ref,
    edge_ref,
    send_ref,
    recv_ref,
    live_ref,
    list_ref,
    recv_row_hbm,
    ew1_hbm,
    eb1_hbm,
    ew2_hbm,
    eg_hbm,
    nw1_hbm,
    nb1_hbm,
    nw2_hbm,
    ng_hbm,
    node_out_ref,
    edge_out_ref,
    recv_row_ref,
    ew1_ref,
    eb1_ref,
    ew2_ref,
    eg_ref,
    nw1_ref,
    nb1_ref,
    nw2_ref,
    ng_ref,
    table_ref,
    face_ref,
    lists_ref,
    mid_ref,
    s_ref,
    r_ref,
    pre_ref,
    msg_ref,
    part_ref,
    pair_ref,
    sums_ref,
    got_ref,
    sum_ref,
    node_ref,
    block_send,
    block_recv,
    list_sem,
    pair_sem,
    sum_sem,
    local_sem,
    load_sem,
):
    d = lax.axis_index("dom")
    e = lax.axis_index("edge")
    doms = lax.axis_size("dom")
    count = lax.axis_size("edge")
    chips = count // 2
    last = chips - 1
    stride = doms // 4
    size, width = own_ref.shape
    half = width // 2
    edges = edge_ref.shape[0]
    nodes = count * size
    parts = size // HALO
    q = e // 2
    c = e % 2
    sib = (d, 2 * q + 1 - c)
    ups = (d, e + 2)
    downs = (d, e - 2)
    there = [(d + s) % doms for s in (1, doms - 1, stride, doms - stride)]

    def peer(t):
        return 2 * ((q + t) % chips) + c

    def loads():
        pairs = (
            (ew1_hbm, ew1_ref),
            (eb1_hbm, eb1_ref),
            (ew2_hbm, ew2_ref),
            (eg_hbm, eg_ref),
            (recv_row_hbm, recv_row_ref),
            (nw1_hbm, nw1_ref),
            (nb1_hbm, nb1_ref),
            (nw2_hbm, nw2_ref),
            (ng_hbm, ng_ref),
        )
        return [
            pltpu.make_async_copy(src, dst, load_sem.at[i]) for i, (src, dst) in enumerate(pairs)
        ]

    def edge_load():
        return pltpu.make_async_copy(edge_ref, mid_ref, local_sem.at[0])

    for load in loads():
        load.start()
    edge_load().start()

    barrier = pltpu.get_barrier_semaphore()

    def greet(who):
        pl.semaphore_signal(barrier, inc=1, device_id=who, device_id_type=MESH)

    greet(sib)
    for t in range(1, chips):
        greet((d, peer(t)))
    for f in (2, 3):
        greet((there[f], e))
    for f in (0, 1):
        greet((there[f], 2 * (last - q) + c))
    pl.semaphore_wait(barrier, 1 + (chips - 1) + 2 + 2)

    def edge_store():
        return pltpu.make_async_copy(mid_ref, edge_out_ref, local_sem.at[1])

    def list_copy(t):
        return pltpu.make_async_remote_copy(
            src_ref=list_ref,
            dst_ref=lists_ref.at[pl.ds(q, 1)],
            send_sem=list_sem.at[0, t],
            recv_sem=list_sem.at[1, t],
            device_id=(d, peer(t)),
            device_id_type=MESH,
        )

    lists_ref[pl.ds(q, 1)] = list_ref[...]
    for t in range(1, chips):
        list_copy(t).start()
    node_ref[...] = own_ref[...]

    def exchange(l):
        def node_block(s, h, core=c):
            return (2 * s + core) * parts + h

        def halo_block(s, f, core=c):
            return count * parts + (2 * s + core) * FACES + f

        def block_at(block):
            return table_ref.at[l, rows(block * HALO, HALO), :]

        def copy(kind, block, who, src=None):
            return pltpu.make_async_remote_copy(
                src_ref=block_at(block) if src is None else src,
                dst_ref=block_at(block),
                send_sem=block_send.at[l, kind, block],
                recv_sem=block_recv.at[l, block],
                device_id=who,
                device_id_type=MESH,
            )

        def start(cond, kind, block, who):
            if cond is None:
                copy(kind, block, who).start()
            else:
                pl.when(cond)(lambda: copy(kind, block, who).start())

        def wait(block):
            copy(SIDE, block, sib).wait_recv()

        ids = lax.broadcasted_iota(jnp.int32, (size, HALO), 0)

        def pick(s, f, who):
            hit = jnp.where(ids == lists_ref[s, pl.ds(f, 1), :], 1.0, 0.0).astype(BF16)
            values = table_ref[l, rows((2 * s + c) * size, size), :]
            face_ref[l, s, f] = lax.dot_general(
                hit, values, (((0,), (0,)), ((), ())), preferred_element_type=F32
            ).astype(BF16)
            copy(ACROSS, halo_block(s, f), who, face_ref.at[l, s, f]).start()

        def at_end(s):
            return ((q == 0) & (s != last)) | ((q == last) & (s != 0))

        def available(s):
            @pl.when(at_end(s))
            def _():
                @pl.loop(0, 2)
                def _(f):
                    pick(s, f, ((d + doms + 1 - 2 * f) % doms, 2 * (last - q) + c))

            @pl.loop(2, FACES)
            def _(f):
                pick(s, f, ((d + doms + stride * (5 - 2 * f)) % doms, e))

        table_ref[l, rows(e * size, size), :] = node_ref[...]
        for h in range(parts):
            start(q < last, UP, node_block(q, h), ups)
            start(q > 0, DOWN, node_block(q, h), downs)
        for h in range(parts):
            start(None, SIDE, node_block(q, h), sib)
        available(q)

        def from_line(s, onward, kind, who):
            for h in range(parts):
                block = node_block(s, h)
                wait(block)
                start(onward, kind, block, who)
                start(None, SIDE, block, sib)

            @pl.when(l == 0)
            def _():
                list_copy((q + chips - s) % chips).wait_recv()

        def from_x(s):
            for f in (2, 3):
                block = halo_block(s, f)
                wait(block)
                start(None, SIDE, block, sib)

        def from_z(s, onward, kind, who):
            for f in (0, 1):
                block = halo_block(s, f)
                wait(block)
                start(onward, kind, block, who)
                start(None, SIDE, block, sib)

        @pl.loop(1, chips + 1)
        def _(k):
            @pl.when((k < chips) & (q >= k))
            def _():
                from_line(q - k, q < last, UP, ups)

            @pl.when((k < chips) & (q + k <= last))
            def _():
                from_line(q + k, q > 0, DOWN, downs)

            @pl.when((k < chips) & (q >= k))
            def _():
                available(q - k)

            @pl.when((k < chips) & (q + k <= last))
            def _():
                available(q + k)

            for kind, who in ((DOWN, downs), (UP, ups)):
                for a, least in enumerate(REACH):
                    place = chips + a - k
                    mine = q if kind == DOWN else last - q
                    s = a if kind == DOWN else last - a

                    @pl.when((mine == place) & (place >= least))
                    def _():
                        from_z(s, place > least, kind, who)

            @pl.when(q >= k - 1)
            def _():
                from_x(q - (k - 1))

            @pl.when((k > 1) & (q + k - 1 <= last))
            def _():
                from_x(q + k - 1)

        def finish_nodes():
            @pl.loop(0, chips)
            def _(s):
                for h in range(parts):
                    wait(node_block(s, h, 1 - c))

        def finish_halo():
            @pl.loop(0, chips)
            def _(s):
                for f in range(FACES):
                    wait(halo_block(s, f, 1 - c))

        def finish_sends():
            for s in range(chips):
                low = REACH[s] if s < last else chips
                high = REACH[last - s] if s else chips
                for h in range(parts):
                    block = node_block(s, h)
                    pl.when((q < last) & (s <= q))(lambda: copy(UP, block, ups).wait_send())
                    pl.when((q > 0) & (s >= q))(lambda: copy(DOWN, block, downs).wait_send())
                    copy(SIDE, block, sib).wait_send()
                for f in range(FACES):
                    block = halo_block(s, f)
                    across = copy(ACROSS, block, sib, face_ref.at[l, s, f])
                    copy(SIDE, block, sib).wait_send()
                    if f >= 2:
                        across.wait_send()
                    else:
                        pl.when(at_end(s))(across.wait_send)
                        pl.when(q > low)(lambda: copy(DOWN, block, downs).wait_send())
                        pl.when(last - q > high)(lambda: copy(UP, block, ups).wait_send())

        return finish_nodes, finish_halo, finish_sends

    def project(l, out_ref, part, first, stop, bias):
        @pl.loop(first // STEP, stop // STEP)
        def _(i):
            base = pl.multiple_of(i * STEP, STEP)
            val = dot(
                table_ref[l, pl.ds(base, STEP), :],
                ew1_ref[l, part * width : (part + 1) * width, :],
            )
            if bias is not None:
                val = val + bias
            out_ref[pl.ds(2 * base, STEP, stride=2), :] = val[:, :half]
            out_ref[pl.ds(2 * base + 1, STEP, stride=2), :] = val[:, half:]

    def edge_phase(l):
        @pl.loop(0, edges // GROUP)
        def _(g):
            for u in range(GROUP):
                k = g * GROUP + u
                a = send_ref[k]
                b = recv_ref[k]
                at = pl.multiple_of(g * (2 * GROUP), 2 * GROUP) + 2 * u
                pre_ref[pl.ds(at, 2), :] = s_ref[pl.ds(2 * a, 2), :] + r_ref[pl.ds(2 * b, 2), :]

        pl.when(l == 0)(lambda: edge_load().wait())
        live = live_ref[0, 0]

        @pl.loop(0, edges // CHUNK)
        def _(i):
            base = pl.multiple_of(i * CHUNK, CHUNK)
            old = mid_ref[pl.ds(base, CHUNK), :]
            pre = dot(old, ew1_ref[l, :width, :])
            low = pre[:, :half] + pre_ref[pl.ds(2 * base, CHUNK, stride=2), :]
            high = pre[:, half:] + pre_ref[pl.ds(2 * base + 1, CHUNK, stride=2), :]
            hidden = jnp.maximum(jnp.concatenate([low, high], axis=1), 0.0).astype(BF16)
            message = layer_norm(dot(hidden, ew2_ref[l]), eg_ref[pl.ds(l, 1), :])
            slot = lax.broadcasted_iota(jnp.int32, (CHUNK, 1), 0) + base
            message = jnp.where(slot < live, message, 0.0)
            mid_ref[pl.ds(base, CHUNK), :] = (old.astype(F32) + message).astype(BF16)
            msg_ref[pl.ds(base, CHUNK), :] = message.astype(BF16)

        pl.when(l == LAYERS - 1)(lambda: edge_store().start())

    def scatter(owner):
        depth = 512
        ids = lax.broadcasted_iota(jnp.int32, (size, depth), 0) + owner * size
        acc = jnp.zeros((size, width), F32)
        for j in range(0, edges, depth):
            hit = ids == recv_row_ref[:, j : j + depth]
            acc = acc + dot(jnp.where(hit, 1.0, 0.0).astype(BF16), msg_ref[j : j + depth, :])
        return acc

    def reduce_phase(l, finish_sends):
        def pair_copy(t):
            return pltpu.make_async_remote_copy(
                src_ref=part_ref.at[l, t],
                dst_ref=pair_ref.at[l, t],
                send_sem=pair_sem.at[l, 0, t],
                recv_sem=pair_sem.at[l, 1, t],
                device_id=sib,
                device_id_type=MESH,
            )

        def sum_copy(t):
            return pltpu.make_async_remote_copy(
                src_ref=sums_ref.at[l, t],
                dst_ref=got_ref.at[l, t],
                send_sem=sum_sem.at[l, 0, t],
                recv_sem=sum_sem.at[l, 1, t],
                device_id=(d, peer(t)),
                device_id_type=MESH,
            )

        def turn(i):
            return (1 - i // 2) * (2 - i) + (i // 2) * (9 - 3 * i)

        def give(t):
            part_ref[l, t] = scatter(2 * ((q + t) % chips) + 1 - c).astype(BF16)
            pair_copy(t).start()

        def gain(t):
            total = scatter(peer(t))
            pair_copy(t).wait_recv()
            total = total + pair_ref[l, t].astype(F32)
            sum_ref[...] = total
            sums_ref[l, t] = total.astype(BF16)
            pl.when(t > 0)(lambda: sum_copy(t).start())

        give(2)

        @pl.loop(1, chips)
        def _(i):
            give(turn(i))
            gain(turn(i - 1))

        gain(0)
        finish_sends()
        own = node_ref[...]
        mine = sum_ref[...]
        pre = dot(own, nw1_ref[l, :width, :]) + nb1_ref[pl.ds(l, 1), :]
        for t in range(1, chips):
            sum_copy(t).wait_recv()
            mine = mine + got_ref[l, t].astype(F32)
        pre = pre + dot(mine.astype(BF16), nw1_ref[l, width:, :])
        hidden = jnp.maximum(pre, 0.0).astype(BF16)
        update = layer_norm(dot(hidden, nw2_ref[l]), ng_ref[pl.ds(l, 1), :])
        node_ref[...] = (own.astype(F32) + update).astype(BF16)
        for t in range(chips):
            pair_copy(t).wait_send()
            if t:
                sum_copy(t).wait_send()

    @pl.loop(0, LAYERS)
    def _(l):
        finish_nodes, finish_halo, finish_sends = exchange(l)
        finish_nodes()

        @pl.when(l == 0)
        def _():
            for load in loads():
                load.wait()

        project(l, s_ref, 1, 0, nodes, None)
        project(l, r_ref, 2, 0, nodes, eb1_ref[pl.ds(l, 1), :])
        finish_halo()
        project(l, s_ref, 1, nodes, table_ref.shape[1], None)
        edge_phase(l)
        reduce_phase(l, finish_sends)

    node_out_ref[...] = node_ref[...]
    edge_store().wait()
    for t in range(1, chips):
        list_copy(t).wait_send()


def settle_kernel(node_ref, edge_ref, node_out_ref, edge_out_ref, node_buf, edge_buf, sems):
    pieces = 4
    size = edge_ref.shape[0] // pieces
    moves = [(node_ref, node_buf, node_out_ref)]
    for i in range(pieces):
        part = pl.ds(i * size, size)
        moves.append((edge_ref.at[part], edge_buf.at[part], edge_out_ref.at[part]))
    loads = [
        pltpu.make_async_copy(move[0], move[1], sems.at[0, i]) for i, move in enumerate(moves)
    ]
    stores = [
        pltpu.make_async_copy(move[1], move[2], sems.at[1, i]) for i, move in enumerate(moves)
    ]
    for load in loads:
        load.start()
    for load, store in zip(loads, stores):
        load.wait()
        store.start()
    for store in stores:
        store.wait()


def shards(
    node_lat,
    edge_lat,
    senders,
    receivers,
    live_edges,
    send_rows,
    edge_w1,
    edge_b1,
    edge_w2,
    edge_gain,
    node_w1,
    node_b1,
    node_w2,
    node_gain,
):
    vmem = pl.BlockSpec(memory_space=pltpu.VMEM)
    smem = pl.BlockSpec(memory_space=pltpu.SMEM)
    hbm = pl.BlockSpec(memory_space=pl.ANY)
    dma = pltpu.SemaphoreType.DMA
    size, width = node_lat.shape
    edges = edge_lat.shape[0]
    count = lax.axis_size("edge")
    chips = count // 2
    nodes = count * size
    table = count * (size + FACES * HALO)
    blocks = table // HALO
    half = width // 2
    weights = (edge_w1, edge_b1, edge_w2, edge_gain, node_w1, node_b1, node_w2, node_gain)
    sums = pltpu.VMEM((LAYERS, chips, size, width), BF16)
    outs = (
        jax.ShapeDtypeStruct(node_lat.shape, BF16),
        jax.ShapeDtypeStruct(edge_lat.shape, BF16),
    )
    own, moved = pl.pallas_call(
        kernel,
        out_shape=outs,
        in_specs=[vmem, hbm, smem, smem, smem, vmem] + [hbm] * 9,
        out_specs=(vmem, hbm),
        scratch_shapes=[
            pltpu.VMEM((1, edges), jnp.int32),
            *(pltpu.VMEM(value.shape, value.dtype) for value in weights),
            pltpu.VMEM((LAYERS, table, width), BF16),
            pltpu.VMEM((LAYERS, chips, FACES, HALO, width), BF16),
            pltpu.VMEM((chips, FACES, HALO), jnp.int32),
            pltpu.VMEM((edges, width), BF16),
            pltpu.VMEM((2 * table, half), F32),
            pltpu.VMEM((2 * nodes, half), F32),
            pltpu.VMEM((2 * edges, half), F32),
            pltpu.VMEM((edges, width), BF16),
            sums,
            sums,
            sums,
            sums,
            pltpu.VMEM((size, width), F32),
            pltpu.VMEM((size, width), BF16),
            dma((LAYERS, 4, blocks)),
            dma((LAYERS, blocks)),
            dma((2, chips)),
            dma((LAYERS, 2, chips)),
            dma((LAYERS, 2, chips)),
            dma((2,)),
            dma((1 + len(weights),)),
        ],
        compiler_params=pltpu.CompilerParams(
            collective_id=0, has_side_effects=True, vmem_limit_bytes=56 * 2**20
        ),
        cost_estimate=pl.CostEstimate(
            flops=2 * 10**10, bytes_accessed=8 * 2**20, transcendentals=0
        ),
        name="graph_layers",
    )(
        node_lat,
        edge_lat,
        senders,
        receivers,
        live_edges,
        send_rows,
        receivers.reshape(1, -1),
        edge_w1,
        edge_b1,
        edge_w2,
        edge_gain,
        node_w1,
        node_b1,
        node_w2,
        node_gain,
    )
    return pl.pallas_call(
        settle_kernel,
        out_shape=outs,
        in_specs=[hbm, hbm],
        out_specs=(hbm, hbm),
        scratch_shapes=[
            pltpu.VMEM(node_lat.shape, BF16),
            pltpu.VMEM(edge_lat.shape, BF16),
            dma((2, 5)),
        ],
        name="settle",
    )(own, moved)


def solution(mesh):
    split = P(("dom", "edge"), None)
    in_specs = (
        split,
        split,
        P(("dom", "edge")),
        P(("dom", "edge")),
        P("dom", "edge"),
        P(("dom", "edge"), None, None),
    ) + (P(),) * 8
    return jax.shard_map(
        shards, mesh=mesh, in_specs=in_specs, out_specs=(split, split), check_vma=False
    )
```
